128 devices in a mesh: grp: 4 (over y), neg: 32 (over z, x, core).
Axes of the slice: x: 4, y: 4, z: 4, core: 2. Of those that a mesh axis runs over, the one named last changes fastest.
Arguments:
- quotient: bfloat16 [1048576, 256], P(('grp', 'neg')), may hold values from -3 to 3
- remainder: bfloat16 [20480, 256], P(('grp', 'neg')), may hold values from -3 to 3
- request_q: int32 [128, 128, 80], P(('grp', 'neg')), may hold values from -1 to 8191, as said below
- request_r: int32 [128, 128, 24], P(('grp', 'neg')), may hold values from -1 to 159, as said below
- query_q: int32 [32768, 16], P(('grp', 'neg')), may hold values from 0 to 10239, as said below
- query_r: int32 [32768, 16], P(('grp', 'neg')), may hold values from 0 to 3071, as said below
- item_q: int32 [32768, 16], P(('grp', 'neg')), may hold values from 0 to 10239, as said below
- item_r: int32 [32768, 16], P(('grp', 'neg')), may hold values from 0 to 3071, as said below
- positive: int32 [32768], P(('grp', 'neg')), may hold values from 0 to 8191
- query_w1: bfloat16 [256, 1024], replicated, may hold values from -0.375 to 0.375
- query_w2: bfloat16 [1024, 1024], replicated, may hold values from -0.1875 to 0.1875
- query_w3: bfloat16 [1024, 256], replicated, may hold values from -0.1875 to 0.1875
- item_w1: bfloat16 [256, 1024], replicated, may hold values from -0.375 to 0.375
- item_w2: bfloat16 [1024, 1024], replicated, may hold values from -0.1875 to 0.1875
- item_w3: bfloat16 [1024, 256], replicated, may hold values from -0.1875 to 0.1875
Outputs:
- grad_quotient: float32 [1048576, 256], P(('grp', 'neg'))
- grad_remainder: float32 [20480, 256], P(('grp', 'neg'))
- grad_query_w1: bfloat16 [256, 1024], replicated
- grad_query_w2: bfloat16 [1024, 1024], replicated
- grad_query_w3: bfloat16 [1024, 256], replicated
- grad_item_w1: bfloat16 [256, 1024], replicated
- grad_item_w2: bfloat16 [1024, 1024], replicated
- grad_item_w3: bfloat16 [1024, 256], replicated
The draws below stay inside these ranges and needn't reach their ends.
Inputs may be any that keep to these rules, and one draw needn't show every extreme that they name: `request_q`: for device d and owner p, the first c(d, p) slots hold distinct rows of owner p's shard and the rest hold -1; c(d, p) runs from 26 to 80; in every draw one owner gets 80 rows from every device, and every device asks 80 rows of some owner. `request_r`: for device d and owner p, the first c(d, p) slots hold distinct rows of owner p's shard and the rest hold -1; c(d, p) runs from 1 to 24; in every draw one owner gets 24 rows from every device, and every device asks 24 rows of some owner. `query_q`: entry p * 80 + k names slot k of owner p in request_q of the device holding the example, and that slot is not -1. `query_r`: entry p * 24 + k names slot k of owner p in request_r of the device holding the example, and that slot is not -1. `item_q`: as for query_q. `item_r`: as for query_r.
All inputs are finite; a program needn't handle non-finite values.
Results may differ from the reference program's by a relative error of at most 0.023.
Values may be sent and summed in bfloat16 or wider, within the bound.
No kernel may reach another device: no remote copies, remote signals or barrier semaphores. Data moves between devices by JAX's collectives and lax.ppermute only.
A program may use at most 128 MiB of HBM per device.

```python
import jax
import jax.numpy as jnp
from jax import lax

E = 256
H = 1024
BAG = 16
B_DEV = 256
Q_DEV = 8192
R_DEV = 160
CAPQ = 80
CAPR = 24
EXAMPLES = 32768
GROUP = 8192
Q_ROWS = 1048576
R_ROWS = 20480
N_GRP = 4
N_NEG = 32
DEVICES = 128


def owner_counts(key, capacity, lowest_level, floor_count):
    devices = DEVICES
    key_level, key_draw, key_own = jax.random.split(key, 3)
    owner_level = jax.random.randint(key_level, (1, devices), lowest_level, capacity + 1)
    spread = jax.random.randint(key_draw, (devices, devices), 0, 1 << 20)
    counts = floor_count + spread % (owner_level - floor_count + 1)
    hottest = devices - 1
    chosen = jax.random.randint(key_own, (devices, 1), 0, devices)
    owners = jnp.arange(devices, dtype=jnp.int32)[None, :]
    counts = jnp.where(owners == hottest, capacity, counts)
    counts = jnp.where(owners == chosen, capacity, counts)
    return counts


def quotient_counts(key):
    return owner_counts(jax.random.fold_in(key, 501), CAPQ, CAPQ, max(1, CAPQ // 3))


def remainder_counts(key):
    return owner_counts(jax.random.fold_in(key, 502), CAPR, 1, 1)


def request_rows(key, counts, capacity, shard_rows):
    devices = DEVICES
    key_anchor, key_stride = jax.random.split(key)
    anchor = jax.random.randint(key_anchor, (devices, devices, 1), 0, shard_rows)
    stride = 10 * jax.random.randint(key_stride, (devices, devices, 1), 0, shard_rows) + 1
    position = jnp.arange(capacity, dtype=jnp.int32)[None, None, :]
    picked = (anchor + position * stride) % shard_rows
    return jnp.where(position < counts[:, :, None], picked, -1)


def bag_slots(key, counts, capacity):
    key_owner, key_slot = jax.random.split(key)
    owner_index = jax.random.randint(key_owner, (EXAMPLES, BAG), 0, DEVICES)
    device = (jnp.arange(EXAMPLES, dtype=jnp.int32) // B_DEV)[:, None]
    live_count = counts[device, owner_index]
    offset = jax.random.randint(key_slot, (EXAMPLES, BAG), 0, 1 << 20) % live_count
    slots = owner_index * capacity + offset
    local_row = (jnp.arange(EXAMPLES, dtype=jnp.int32) % B_DEV)[:, None]
    position = jnp.arange(BAG, dtype=jnp.int32)[None, :]
    slots = jnp.where((local_row == 0) & (position == 0), DEVICES * capacity - 1, slots)
    slots = jnp.where((local_row == 1) & (position == 0), 0, slots)
    return slots


def draw_request_q(key, part):
    counts = quotient_counts(key)
    key = jax.random.fold_in(key, 11)
    return request_rows(key, counts, CAPQ, Q_DEV)


def draw_request_r(key, part):
    counts = remainder_counts(key)
    key = jax.random.fold_in(key, 12)
    return request_rows(key, counts, CAPR, R_DEV)


def draw_query_q(key, part):
    counts = quotient_counts(key)
    key = jax.random.fold_in(key, 13)
    return bag_slots(key, counts, CAPQ)


def draw_query_r(key, part):
    counts = remainder_counts(key)
    key = jax.random.fold_in(key, 14)
    return bag_slots(key, counts, CAPR)


def draw_item_q(key, part):
    counts = quotient_counts(key)
    key = jax.random.fold_in(key, 15)
    return bag_slots(key, counts, CAPQ)


def draw_item_r(key, part):
    counts = remainder_counts(key)
    key = jax.random.fold_in(key, 16)
    return bag_slots(key, counts, CAPR)


def set_ends(array, key, least, largest):
    place = [jax.random.randint(jax.random.fold_in(key, axis), (), 0, length) for axis, length in enumerate(array.shape)]
    longest = array.shape.index(max(array.shape))
    neighbour = place[:longest] + [(place[longest] + 1) % array.shape[longest]] + place[longest + 1:]
    return array.at[tuple(place)].set(least).at[tuple(neighbour)].set(largest)


def block_levels(stream_key, extent, cuts, smallest, top_value):
    factor_of, own = 1.0, jax.random.fold_in(stream_key, 6)
    for dim, blocks in cuts:
        draws = jnp.exp(jax.random.uniform(jax.random.fold_in(own, dim), (blocks,), jnp.float32, smallest / len(cuts), top_value / len(cuts)))
        factor_of = factor_of * jnp.repeat(draws, extent[dim] // blocks).reshape([-1 if axis == dim else 1 for axis in range(len(extent))])
    return factor_of


def gaussian(key, dims, deviation, most, cuts=(), held_as=jnp.bfloat16):
    array = deviation * jax.random.normal(key, dims, jnp.float32)
    if cuts:
        array = array * block_levels(key, dims, cuts, -0.22, 0.18)
    return jnp.clip(array, -most, most).astype(held_as)


def setup_inputs(seed: int = 0) -> dict:
    splits = jax.random.split(jax.random.key(seed), 16)
    quotient = gaussian(splits[0], (Q_ROWS, E), 0.5, 3.0, ((0, 128),))
    remainder = gaussian(splits[1], (R_ROWS, E), 0.5, 3.0, ((0, 128),))
    request_q = draw_request_q(jax.random.fold_in(splits[15], 71), 0)
    request_r = draw_request_r(jax.random.fold_in(splits[15], 71), 0)
    query_q = draw_query_q(jax.random.fold_in(splits[15], 71), 0)
    query_r = draw_query_r(jax.random.fold_in(splits[15], 71), 0)
    item_q = draw_item_q(jax.random.fold_in(splits[15], 71), 0)
    item_r = draw_item_r(jax.random.fold_in(splits[15], 71), 0)
    positive = set_ends(jax.random.randint(splits[8], (EXAMPLES,), 0, GROUP), jax.random.fold_in(splits[8], 1), 0, GROUP - 1).astype(jnp.int32)
    query_w1 = gaussian(splits[9], (E, H), E ** -0.5, 0.375)
    query_w2 = gaussian(splits[10], (H, H), H ** -0.5, 0.1875)
    query_w3 = gaussian(splits[11], (H, E), H ** -0.5, 0.1875)
    item_w1 = gaussian(splits[12], (E, H), E ** -0.5, 0.375)
    item_w2 = gaussian(splits[13], (H, H), H ** -0.5, 0.1875)
    item_w3 = gaussian(splits[14], (H, E), H ** -0.5, 0.1875)
    return dict(quotient=quotient, remainder=remainder, request_q=request_q, request_r=request_r, query_q=query_q, query_r=query_r, item_q=item_q, item_r=item_r, positive=positive, query_w1=query_w1, query_w2=query_w2, query_w3=query_w3, item_w1=item_w1, item_w2=item_w2, item_w3=item_w3)


SCALE = 20.0
EPS = 1e-06

def inner(left, right):
    return lax.dot_general(left, right, (((0,), (0,)), ((), ())), preferred_element_type=jnp.float32)

def outer_t(left, right):
    return lax.dot_general(left, right, (((1,), (1,)), ((), ())), preferred_element_type=jnp.float32)

def gelu_back(pre_value, upstream):
    return jax.vjp(jax.nn.gelu, pre_value)[1](upstream)[0]

def tower_forward(pooled, first, second, third):
    pre_one = jnp.dot(pooled, first, preferred_element_type=jnp.float32)
    act_one = jax.nn.gelu(pre_one).astype(jnp.bfloat16)
    pre_two = jnp.dot(act_one, second, preferred_element_type=jnp.float32)
    act_two = jax.nn.gelu(pre_two).astype(jnp.bfloat16)
    vector = jnp.dot(act_two, third, preferred_element_type=jnp.float32)
    inv_norm = lax.rsqrt(lax.optimization_barrier(jnp.sum(vector * vector, axis=1, keepdims=True)) + EPS)
    unit_vec = (vector * inv_norm).astype(jnp.bfloat16)
    return (unit_vec, (pre_one, act_one, pre_two, act_two, vector, inv_norm))

def tower_backward(d_unit, saved, pooled, first, second, third):
    pre_one, act_one, pre_two, act_two, vector, inv_norm = saved
    along = lax.optimization_barrier(jnp.sum(vector * d_unit, axis=1, keepdims=True))
    cubed = inv_norm * inv_norm * inv_norm
    d_vector = (inv_norm * d_unit - cubed * vector * along).astype(jnp.bfloat16)
    grad_third = inner(act_two, d_vector)
    d_pre_two = gelu_back(pre_two, outer_t(d_vector, third)).astype(jnp.bfloat16)
    grad_second = inner(act_one, d_pre_two)
    d_pre_one = gelu_back(pre_one, outer_t(d_pre_two, second)).astype(jnp.bfloat16)
    grad_first = inner(pooled, d_pre_one)
    d_pooled = outer_t(d_pre_one, first)
    return ((grad_first, grad_second, grad_third), d_pooled)

def score_grads(query_unit, item_unit, positive):
    scores = SCALE * outer_t(query_unit, item_unit)
    weights = jnp.exp(scores - SCALE)
    probs = weights / lax.optimization_barrier(jnp.sum(weights, axis=1, keepdims=True))
    columns = jnp.arange(item_unit.shape[0], dtype=jnp.int32)[None, :]
    target = (positive[:, None] == columns).astype(jnp.float32)
    return (probs - target).astype(jnp.bfloat16)

def fetch(table, request, shard_rows):
    owners = jnp.arange(request.shape[0], dtype=jnp.int32)[:, None] * shard_rows
    picked = jnp.take(table, jnp.maximum(request, 0) + owners, axis=0)
    picked = jnp.where((request >= 0)[:, :, None], picked, jnp.zeros((), table.dtype))
    return picked.reshape(-1, table.shape[1])

def pool_rows(fetched_q, fetched_r, slots_q, slots_r):
    rows_q = jnp.take(fetched_q, slots_q, axis=0)
    rows_r = jnp.take(fetched_r, slots_r, axis=0)
    product = rows_q.astype(jnp.float32) * rows_r.astype(jnp.float32)
    return lax.optimization_barrier(jnp.sum(product, axis=1)).astype(jnp.bfloat16)

def reference(quotient, remainder, request_q, request_r, query_q, query_r, item_q, item_r, positive, query_w1, query_w2, query_w3, item_w1, item_w2, item_w3):
    features = quotient.shape[1]

    def by_device(values):
        return values.reshape(DEVICES, B_DEV, BAG)

    def pool_device(pieces):
        ask_q, ask_r, slots_qq, slots_qr, slots_iq, slots_ir = pieces
        table_q = fetch(quotient, ask_q, Q_DEV)
        table_r = fetch(remainder, ask_r, R_DEV)
        return (pool_rows(table_q, table_r, slots_qq, slots_qr), pool_rows(table_q, table_r, slots_iq, slots_ir))
    pooled_query, pooled_item = lax.map(pool_device, (request_q, request_r, by_device(query_q), by_device(query_r), by_device(item_q), by_device(item_r)))
    pooled_query = pooled_query.reshape(EXAMPLES, features)
    pooled_item = pooled_item.reshape(EXAMPLES, features)
    query_unit, query_saved = tower_forward(pooled_query, query_w1, query_w2, query_w3)
    item_unit, item_saved = tower_forward(pooled_item, item_w1, item_w2, item_w3)

    def group_grads(pieces):
        group_query, group_item, group_positive = pieces
        dscore = score_grads(group_query, group_item, group_positive)
        d_query = SCALE * jnp.dot(dscore, group_item, preferred_element_type=jnp.float32)

        def add_device(member, total):
            first_row = (member * B_DEV).astype(jnp.int32)
            score_rows = lax.dynamic_slice_in_dim(dscore, first_row, B_DEV, 0)
            own_query = lax.dynamic_slice_in_dim(group_query, first_row, B_DEV, 0)
            term = (SCALE * inner(score_rows, own_query)).astype(jnp.bfloat16)
            term = lax.optimization_barrier(term)
            return total + term.astype(jnp.float32)
        d_item = lax.fori_loop(0, N_NEG, add_device, jnp.zeros((GROUP, features), jnp.float32))
        return (d_query, d_item)
    d_query, d_item = lax.map(group_grads, (query_unit.reshape(N_GRP, GROUP, features), item_unit.reshape(N_GRP, GROUP, features), positive.reshape(N_GRP, GROUP)))
    d_query = d_query.reshape(EXAMPLES, features)
    d_item = d_item.reshape(EXAMPLES, features)
    query_grads, query_back = tower_backward(d_query, query_saved, pooled_query, query_w1, query_w2, query_w3)
    item_grads, item_back = tower_backward(d_item, item_saved, pooled_item, item_w1, item_w2, item_w3)

    def add_tables(carry, pieces):
        grad_q, grad_r = carry
        ask_q, ask_r, slots_qq, slots_qr, slots_iq, slots_ir, back_query, back_item = pieces
        table_q = fetch(quotient, ask_q, Q_DEV)
        table_r = fetch(remainder, ask_r, R_DEV)
        slots_q = jnp.concatenate([slots_qq, slots_iq], axis=0)
        slots_r = jnp.concatenate([slots_qr, slots_ir], axis=0)
        back_all = jnp.concatenate([back_query, back_item], axis=0)[:, None, :]
        rows_q = jnp.take(table_q, slots_q, axis=0).astype(jnp.float32)
        rows_r = jnp.take(table_r, slots_r, axis=0).astype(jnp.float32)
        sums_q = jax.ops.segment_sum((back_all * rows_r).reshape(-1, features), slots_q.reshape(-1), num_segments=table_q.shape[0])
        sums_r = jax.ops.segment_sum((back_all * rows_q).reshape(-1, features), slots_r.reshape(-1), num_segments=table_r.shape[0])
        owners = jnp.arange(DEVICES, dtype=jnp.int32)[:, None]
        target_q = jnp.where(ask_q >= 0, ask_q + owners * Q_DEV, Q_ROWS).reshape(-1)
        target_r = jnp.where(ask_r >= 0, ask_r + owners * R_DEV, R_ROWS).reshape(-1)
        grad_q = grad_q.at[target_q].add(sums_q, mode='drop')
        grad_r = grad_r.at[target_r].add(sums_r, mode='drop')
        return ((grad_q, grad_r), None)
    start = (jnp.zeros((Q_ROWS, features), jnp.float32), jnp.zeros((R_ROWS, features), jnp.float32))
    (grad_quotient, grad_remainder), _ = lax.scan(add_tables, start, (request_q, request_r, by_device(query_q), by_device(query_r), by_device(item_q), by_device(item_r), query_back.reshape(DEVICES, B_DEV, features), item_back.reshape(DEVICES, B_DEV, features)))
    return (grad_quotient, grad_remainder, query_grads[0].astype(jnp.bfloat16), query_grads[1].astype(jnp.bfloat16), query_grads[2].astype(jnp.bfloat16), item_grads[0].astype(jnp.bfloat16), item_grads[1].astype(jnp.bfloat16), item_grads[2].astype(jnp.bfloat16))
```

```python
import jax
import jax.numpy as jnp
from jax import lax
from jax.experimental import pallas as pl
from jax.experimental.pallas import tpu as pltpu
from jax.sharding import PartitionSpec as P

SCALE = 20.0
EPS = 1e-06
MESH_AXES = ("grp", "neg")
VMEM_LIMIT = 56 * 1024 * 1024
LANES = 16


def inner(left, right):
    return lax.dot_general(
        left, right, (((0,), (0,)), ((), ())), preferred_element_type=jnp.float32
    )


def outer_t(left, right):
    return lax.dot_general(
        left, right, (((1,), (1,)), ((), ())), preferred_element_type=jnp.float32
    )


def gelu_back(pre_value, upstream):
    return jax.vjp(jax.nn.gelu, pre_value)[1](upstream)[0]


def tower_forward(pooled, first, second, third):
    pre_one = jnp.dot(pooled, first, preferred_element_type=jnp.float32)
    act_one = jax.nn.gelu(pre_one).astype(jnp.bfloat16)
    pre_two = jnp.dot(act_one, second, preferred_element_type=jnp.float32)
    act_two = jax.nn.gelu(pre_two).astype(jnp.bfloat16)
    vector = jnp.dot(act_two, third, preferred_element_type=jnp.float32)
    inv_norm = lax.rsqrt(jnp.sum(vector * vector, axis=1, keepdims=True) + EPS)
    unit_vec = (vector * inv_norm).astype(jnp.bfloat16)
    return (unit_vec, (pre_one, act_one, pre_two, act_two, vector, inv_norm))


def tower_backward(d_unit, saved, pooled, first, second, third):
    pre_one, act_one, pre_two, act_two, vector, inv_norm = saved
    along = jnp.sum(vector * d_unit, axis=1, keepdims=True)
    cubed = inv_norm * inv_norm * inv_norm
    d_vector = (inv_norm * d_unit - cubed * vector * along).astype(jnp.bfloat16)
    grad_third = inner(act_two, d_vector)
    d_pre_two = gelu_back(pre_two, outer_t(d_vector, third)).astype(jnp.bfloat16)
    grad_second = inner(act_one, d_pre_two)
    d_pre_one = gelu_back(pre_one, outer_t(d_pre_two, second)).astype(jnp.bfloat16)
    grad_first_t = inner(d_pre_one, pooled)
    d_pooled = outer_t(d_pre_one, first)
    grads = jnp.concatenate(
        [g.astype(jnp.bfloat16) for g in (grad_second, grad_third, grad_first_t)], axis=1
    )
    return (grads, d_pooled)


def score_weights(left, right):
    return jnp.exp(SCALE * outer_t(left, right) - SCALE)


def gather_group(values):
    return lax.all_gather(values, "neg", axis=0, tiled=True)


def exchange(rows):
    return lax.all_to_all(rows, MESH_AXES, split_axis=0, concat_axis=0, tiled=True)


def widen(narrow_ref, wide_ref):
    step = 64
    rows = narrow_ref.shape[0]

    def body(block, carry):
        at = pl.ds(pl.multiple_of(block * step, step), step)
        wide_ref[at, :] = narrow_ref[at, :].astype(jnp.float32)
        return carry

    lax.fori_loop(0, rows // step, body, 0)


def whole(space=pltpu.VMEM):
    return pl.BlockSpec(memory_space=space)


def params():
    return pltpu.CompilerParams(vmem_limit_bytes=VMEM_LIMIT)


def pick_kernel(index_ref, table_ref, out_ref, wide_ref, stage_ref):
    chunk = pl.program_id(0)
    rows = out_ref.shape[0]

    @pl.when(chunk == 0)
    def _():
        widen(table_ref, wide_ref)

    group = stage_ref.shape[0]

    def body(part, carry):
        first = chunk * rows + part * group
        for j in range(group):
            stage_ref[pl.ds(j, 1), :] = wide_ref[pl.ds(index_ref[first + j], 1), :]
        at = pl.ds(pl.multiple_of(part * group, group), group)
        out_ref[at, :] = stage_ref[...].astype(jnp.bfloat16)
        return carry

    lax.fori_loop(0, rows // group, body, 0)


def pick_rows(index, table):
    count, (held, features) = index.shape[0], table.shape
    chunk = 1024
    return pl.pallas_call(
        pick_kernel,
        grid=(count // chunk,),
        out_shape=jax.ShapeDtypeStruct((count, features), jnp.bfloat16),
        in_specs=[whole(pltpu.SMEM), whole()],
        out_specs=pl.BlockSpec((chunk, features), lambda i: (i, 0)),
        scratch_shapes=[
            pltpu.VMEM((held, features), jnp.float32),
            pltpu.VMEM((64, features), jnp.float32),
        ],
        compiler_params=params(),
        cost_estimate=pl.CostEstimate(
            flops=count * features, bytes_accessed=4 * count * features, transcendentals=0
        ),
        name="pick_rows",
    )(index, table)


def pool_kernel(slot_q_ref, slot_r_ref, table_q_ref, table_r_ref, out_ref, wide_q, wide_r, stage_ref):
    widen(table_r_ref, wide_r)
    widen(table_q_ref, wide_q)
    examples = out_ref.shape[0]
    bag = slot_q_ref.shape[0] // examples
    group = stage_ref.shape[0]

    def body(part, carry):
        for j in range(group):
            first = (part * group + j) * bag
            terms = [
                wide_q[pl.ds(slot_q_ref[first + l], 1), :]
                * wide_r[pl.ds(slot_r_ref[first + l], 1), :]
                for l in range(bag)
            ]
            while len(terms) > 1:
                terms = [a + b for a, b in zip(terms[::2], terms[1::2], strict=True)]
            stage_ref[pl.ds(j, 1), :] = terms[0]
        at = pl.ds(pl.multiple_of(part * group, group), group)
        out_ref[at, :] = stage_ref[...].astype(jnp.bfloat16)
        return carry

    lax.fori_loop(0, examples // group, body, 0)


def pool_rows(slot_q, slot_r, table_q, table_r, examples):
    features = table_q.shape[1]
    return pl.pallas_call(
        pool_kernel,
        out_shape=jax.ShapeDtypeStruct((examples, features), jnp.bfloat16),
        in_specs=[whole(pltpu.SMEM), whole(pltpu.SMEM), whole(), whole()],
        out_specs=whole(),
        scratch_shapes=[
            pltpu.VMEM(table_q.shape, jnp.float32),
            pltpu.VMEM(table_r.shape, jnp.float32),
            pltpu.VMEM((16, features), jnp.float32),
        ],
        compiler_params=params(),
        cost_estimate=pl.CostEstimate(
            flops=2 * slot_q.shape[0] * features,
            bytes_accessed=2 * (table_q.size + table_r.size),
            transcendentals=0,
        ),
        name="pool_rows",
    )(slot_q, slot_r, table_q, table_r)


def spread_kernel(slot_ref, other_slot_ref, other_ref, back_ref, out_ref, wide_ref, *sums):
    widen(other_ref, wide_ref)
    rows = out_ref.shape[0]
    step = 64

    def clear(block, carry):
        at = pl.ds(pl.multiple_of(block * step, step), step)
        for total in sums:
            total[at, :] = jnp.zeros((step, total.shape[1]), jnp.float32)
        return carry

    lax.fori_loop(0, rows // step, clear, 0)
    examples = back_ref.shape[0]
    bag = slot_ref.shape[0] // examples
    lanes = len(sums)
    share = examples // lanes

    def body(e, carry):
        backs = [back_ref[pl.ds(lane * share + e, 1), :] for lane in range(lanes)]
        for l in range(bag):
            for lane, total in enumerate(sums):
                place = (lane * share + e) * bag + l
                row = pl.ds(slot_ref[place], 1)
                term = backs[lane] * wide_ref[pl.ds(other_slot_ref[place], 1), :]
                total[row, :] = total[row, :] + term
        return carry

    lax.fori_loop(0, share, body, 0)

    def finish(block, carry):
        at = pl.ds(pl.multiple_of(block * step, step), step)
        value = sums[0][at, :]
        for total in sums[1:]:
            value = value + total[at, :]
        out_ref[at, :] = value.astype(jnp.bfloat16)
        return carry

    lax.fori_loop(0, rows // step, finish, 0)


def spread_rows(slot, other_slot, other, back, rows, lanes):
    features = other.shape[1]
    return pl.pallas_call(
        spread_kernel,
        out_shape=jax.ShapeDtypeStruct((rows, features), jnp.bfloat16),
        in_specs=[whole(pltpu.SMEM), whole(pltpu.SMEM), whole(), whole()],
        out_specs=whole(),
        scratch_shapes=[pltpu.VMEM(other.shape, jnp.float32)]
        + [pltpu.VMEM((rows, features), jnp.float32) for _ in range(lanes)],
        compiler_params=params(),
        cost_estimate=pl.CostEstimate(
            flops=2 * slot.shape[0] * features,
            bytes_accessed=2 * (other.size + rows * features),
            transcendentals=0,
        ),
        name="spread_rows",
    )(slot, other_slot, other, back)


def absorb_kernel(index_ref, received_ref, out_ref, wide_ref):
    chunk = pl.program_id(0)
    step = 64

    @pl.when(chunk == 0)
    def _():
        def clear(block, carry):
            at = pl.ds(pl.multiple_of(block * step, step), step)
            out_ref[at, :] = jnp.zeros((step, out_ref.shape[1]), jnp.float32)
            return carry

        lax.fori_loop(0, out_ref.shape[0] // step, clear, 0)

    widen(received_ref, wide_ref)
    rows = received_ref.shape[0]

    def body(part, carry):
        first = part * LANES
        places = [pl.ds(index_ref[chunk * rows + first + j], 1) for j in range(LANES)]
        values = [
            out_ref[places[j], :] + wide_ref[pl.ds(first + j, 1), :] for j in range(LANES)
        ]
        for j in reversed(range(LANES)):
            out_ref[places[j], :] = values[j]
        return carry

    lax.fori_loop(0, rows // LANES, body, 0)


def absorb_rows(index, received, held):
    count, features = received.shape
    chunk = 1280
    return pl.pallas_call(
        absorb_kernel,
        grid=(count // chunk,),
        out_shape=jax.ShapeDtypeStruct((held, features), jnp.float32),
        in_specs=[whole(pltpu.SMEM), pl.BlockSpec((chunk, features), lambda i: (i, 0))],
        out_specs=whole(),
        scratch_shapes=[pltpu.VMEM((chunk, features), jnp.float32)],
        compiler_params=params(),
        cost_estimate=pl.CostEstimate(
            flops=count * features,
            bytes_accessed=2 * received.size + 4 * held * features,
            transcendentals=0,
        ),
        name="absorb_rows",
    )(index, received)


def local(
    quotient,
    remainder,
    request_q,
    request_r,
    query_q,
    query_r,
    item_q,
    item_r,
    positive,
    query_w1,
    query_w2,
    query_w3,
    item_w1,
    item_w2,
    item_w3,
):
    features = quotient.shape[1]
    capacity_q = request_q.shape[2]
    examples = query_q.shape[0]
    positive_all = gather_group(positive)[None, :]
    asked = exchange(jnp.concatenate([request_q[0], request_r[0]], axis=1))
    asked_q = jnp.maximum(asked[:, :capacity_q], 0).reshape(-1)
    asked_r = asked[:, capacity_q:].reshape(-1)
    shard_r = remainder.shape[0]
    named_r = (asked_r[:, None] == jnp.arange(shard_r, dtype=jnp.int32)[None, :]).astype(
        jnp.bfloat16
    )
    served_r = jnp.dot(named_r, remainder, preferred_element_type=jnp.float32).astype(jnp.bfloat16)
    served_q = pick_rows(asked_q, quotient)
    lists = request_q.shape[1]
    table_r = exchange(served_r.reshape(lists, -1, features)).reshape(-1, features)
    table_q = exchange(served_q.reshape(lists, -1, features)).reshape(-1, features)

    slots_iq, slots_ir = item_q.reshape(-1), item_r.reshape(-1)
    slots_qq, slots_qr = query_q.reshape(-1), query_r.reshape(-1)
    slots_q = jnp.concatenate([slots_qq, slots_iq])
    slots_r = jnp.concatenate([slots_qr, slots_ir])
    pooled = pool_rows(slots_q, slots_r, table_q, table_r, 2 * examples)
    pooled_query, pooled_item = pooled[:examples], pooled[examples:]
    query_unit, query_saved = tower_forward(pooled_query, query_w1, query_w2, query_w3)
    item_unit, item_saved = tower_forward(pooled_item, item_w1, item_w2, item_w3)
    units = jnp.concatenate([item_unit, query_unit], axis=1)
    units, positive_all = lax.optimization_barrier((units, positive_all))
    units_all = gather_group(units)
    items_all, queries_all = units_all[:, :features], units_all[:, features:]

    group = items_all.shape[0]
    columns = jnp.arange(group, dtype=jnp.int32)[None, :]
    weights = score_weights(query_unit, items_all)
    inverse = 1.0 / jnp.sum(weights, axis=1, keepdims=True)
    target = (positive[:, None] == columns).astype(jnp.float32)
    d_query = SCALE * jnp.dot(
        (weights * inverse - target).astype(jnp.bfloat16),
        items_all,
        preferred_element_type=jnp.float32,
    )
    inverse_all = gather_group(inverse[:, 0])[None, :]
    query_grads, query_back = tower_backward(
        d_query, query_saved, pooled_query, query_w1, query_w2, query_w3
    )
    own = lax.axis_index("neg") * examples + jnp.arange(examples, dtype=jnp.int32)
    weights_t = score_weights(item_unit, queries_all)
    target_t = (positive_all == own[:, None]).astype(jnp.float32)
    d_item = SCALE * jnp.dot(
        (weights_t * inverse_all - target_t).astype(jnp.bfloat16),
        queries_all,
        preferred_element_type=jnp.float32,
    )
    query_summed = lax.psum(query_grads, MESH_AXES)
    item_grads, item_back = tower_backward(
        d_item, item_saved, pooled_item, item_w1, item_w2, item_w3
    )
    item_grads, query_summed = lax.optimization_barrier((item_grads, query_summed))
    item_summed = lax.psum(item_grads, MESH_AXES)
    back_all = jnp.concatenate([query_back, item_back], axis=0)
    sums_r = spread_rows(slots_r, slots_q, table_q, back_all, table_r.shape[0], 4)
    back_r = exchange(sums_r.reshape(lists, -1, features)).reshape(-1, features)
    sums_q = spread_rows(slots_q, slots_r, table_r, back_all, table_q.shape[0], 2)
    back_q = exchange(sums_q.reshape(lists, -1, features)).reshape(-1, features)
    grad_remainder = inner(named_r, back_r)
    grad_quotient = absorb_rows(asked_q, back_q, quotient.shape[0])

    hidden = query_w2.shape[0]

    def split(summed):
        return (
            summed[:, hidden + features :].T,
            summed[:, :hidden],
            summed[:, hidden : hidden + features],
        )

    return (grad_quotient, grad_remainder, *split(query_summed), *split(item_summed))


def solution(mesh):
    placed = (
        P(("grp", "neg"), None),
        P(("grp", "neg"), None),
        P(("grp", "neg"), None, None),
        P(("grp", "neg"), None, None),
        P(("grp", "neg"), None),
        P(("grp", "neg"), None),
        P(("grp", "neg"), None),
        P(("grp", "neg"), None),
        P(("grp", "neg")),
        P(),
        P(),
        P(),
        P(),
        P(),
        P(),
    )
    return jax.shard_map(
        local,
        mesh=mesh,
        in_specs=placed,
        out_specs=(P(("grp", "neg"), None), P(("grp", "neg"), None), P(), P(), P(), P(), P(), P()),
        check_vma=False,
    )
```

```python
import functools

import jax
import jax.numpy as jnp
from jax import lax
from jax.experimental import pallas as pl
from jax.experimental.pallas import tpu as pltpu
from jax.sharding import Mesh
from jax.sharding import PartitionSpec as P

SCALE = 20.0
EPS = 1e-06
GROUP_AXES = ("chip", "core")
MESH_AXES = ("grp", "chip", "core")
VMEM_LIMIT = 60 * 1024 * 1024
HALF = 128


def inner(left, right):
    return lax.dot_general(
        left, right, (((0,), (0,)), ((), ())), preferred_element_type=jnp.float32
    )


def outer_t(left, right):
    return lax.dot_general(
        left, right, (((1,), (1,)), ((), ())), preferred_element_type=jnp.float32
    )


def gelu_back(pre_value, upstream):
    return jax.vjp(jax.nn.gelu, pre_value)[1](upstream)[0]


def tower_forward(pooled, first, second, third):
    pre_one = jnp.dot(pooled, first, preferred_element_type=jnp.float32)
    act_one = jax.nn.gelu(pre_one).astype(jnp.bfloat16)
    pre_two = jnp.dot(act_one, second, preferred_element_type=jnp.float32)
    act_two = jax.nn.gelu(pre_two).astype(jnp.bfloat16)
    vector = jnp.dot(act_two, third, preferred_element_type=jnp.float32)
    inv_norm = lax.rsqrt(jnp.sum(vector * vector, axis=1, keepdims=True) + EPS)
    unit_vec = (vector * inv_norm).astype(jnp.bfloat16)
    return (unit_vec, (pre_one, act_one, pre_two, act_two, vector, inv_norm))


def tower_backward(d_unit, saved, pooled, first, second, third):
    pre_one, act_one, pre_two, act_two, vector, inv_norm = saved
    along = jnp.sum(vector * d_unit, axis=1, keepdims=True)
    cubed = inv_norm * inv_norm * inv_norm
    d_vector = (inv_norm * d_unit - cubed * vector * along).astype(jnp.bfloat16)
    grad_third = inner(act_two, d_vector)
    d_pre_two = gelu_back(pre_two, outer_t(d_vector, third)).astype(jnp.bfloat16)
    grad_second = inner(act_one, d_pre_two)
    d_pre_one = gelu_back(pre_one, outer_t(d_pre_two, second)).astype(jnp.bfloat16)
    grad_first_t = inner(d_pre_one, pooled)
    d_pooled = outer_t(d_pre_one, first)
    grads = jnp.concatenate([grad_second, grad_third, grad_first_t], axis=1)
    return (grads, d_pooled)


def score_weights(left, right):
    return jnp.exp(SCALE * outer_t(left, right) - SCALE)


def gather_group(values):
    return lax.all_gather(values, GROUP_AXES, axis=0, tiled=True)


def exchange(rows):
    return lax.all_to_all(rows, MESH_AXES, split_axis=0, concat_axis=0, tiled=True)


def core_sum(grads):
    core, half = lax.axis_index("core"), grads.shape[0] // 2
    kept = lax.dynamic_slice_in_dim(grads, core * half, half, 0)
    given = lax.dynamic_slice_in_dim(grads, (1 - core) * half, half, 0).astype(jnp.bfloat16)
    got = lax.ppermute(given, "core", [(0, 1), (1, 0)])
    chips = lax.axis_size(("grp", "chip"))
    return (kept + got.astype(jnp.float32)).astype(jnp.bfloat16).reshape(chips, half // chips, -1)


def chip_sum(terms):
    terms = lax.all_to_all(terms, ("grp", "chip"), split_axis=0, concat_axis=0, tiled=True)
    return jnp.sum(terms.astype(jnp.float32), axis=0).astype(jnp.bfloat16)


def loop(count, step, body):
    def run(i, carry):
        body(pl.multiple_of(i * step, step))
        return carry
    lax.fori_loop(0, count // step, run, 0)

def widen(narrow_ref, wide_ref):
    def body(first):
        at = pl.ds(first, 64)
        value = narrow_ref[at, :].astype(jnp.float32)
        wide_ref[at, 0, :] = value[:, :HALF]
        wide_ref[at, 1, :] = value[:, HALF:]
    loop(narrow_ref.shape[0], 64, body)

def cost(microseconds):
    return pl.CostEstimate(flops=0, bytes_accessed=int(microseconds * 3.6e6), transcendentals=0)


def whole(space=pltpu.VMEM):
    return pl.BlockSpec(memory_space=space)

def params():
    return pltpu.CompilerParams(vmem_limit_bytes=VMEM_LIMIT)

def joined(ref, at):
    return jnp.concatenate([ref[at, 0, :], ref[at, 1, :]], axis=1)

def pick_kernel(index_ref, table_ref, out_ref, wide_ref, stage_ref):
    chunk = pl.program_id(0)
    rows = out_ref.shape[0]
    @pl.when(chunk == 0)
    def _():
        widen(table_ref, wide_ref)
    group = stage_ref.shape[0]
    def body(first):
        for j in range(group):
            stage_ref[j] = wide_ref[index_ref[chunk * rows + first + j]]
        out_ref[pl.ds(first, group), :] = joined(stage_ref, pl.ds(0, group)).astype(jnp.bfloat16)
    loop(rows, group, body)

def pick_rows(index, table, chunk=1024, group=64):
    count, (held, features) = index.shape[0], table.shape
    return pl.pallas_call(
        pick_kernel, grid=(count // chunk,),
        out_shape=jax.ShapeDtypeStruct((count, features), jnp.bfloat16),
        in_specs=[whole(pltpu.SMEM), whole()],
        out_specs=pl.BlockSpec((chunk, features), lambda i: (i, 0)),
        scratch_shapes=[pltpu.VMEM((held, 2, HALF), jnp.float32), pltpu.VMEM((group, 2, HALF), jnp.float32)],
        compiler_params=params(),
        cost_estimate=cost(20), name="pick_rows")(index, table)

def pool_kernel(slot_q_ref, slot_r_ref, table_q_ref, table_r_ref, out_ref, wide_q, wide_r, stage_ref):
    widen(table_r_ref, wide_r)
    widen(table_q_ref, wide_q)
    examples = out_ref.shape[0]
    bag = slot_q_ref.shape[0] // examples
    group = stage_ref.shape[0]
    def body(first):
        for j in range(group):
            place = (first + j) * bag
            terms = [wide_q[slot_q_ref[place + l]] * wide_r[slot_r_ref[place + l]] for l in range(bag)]
            while len(terms) > 1:
                terms = [a + b for a, b in zip(terms[::2], terms[1::2], strict=True)]
            stage_ref[j] = terms[0]
        out_ref[pl.ds(first, group), :] = joined(stage_ref, pl.ds(0, group)).astype(jnp.bfloat16)
    loop(examples, group, body)

def pool_rows(slot_q, slot_r, table_q, table_r, examples, group=16):
    features = table_q.shape[1]
    return pl.pallas_call(
        pool_kernel,
        out_shape=jax.ShapeDtypeStruct((examples, features), jnp.bfloat16),
        in_specs=[whole(pltpu.SMEM), whole(pltpu.SMEM), whole(), whole()],
        out_specs=whole(),
        scratch_shapes=[pltpu.VMEM((table_q.shape[0], 2, HALF), jnp.float32),
            pltpu.VMEM((table_r.shape[0], 2, HALF), jnp.float32),
            pltpu.VMEM((group, 2, HALF), jnp.float32)],
        compiler_params=params(),
        cost_estimate=cost(28), name="pool_rows")(slot_q, slot_r, table_q, table_r)

def spread_kernel(slot_ref, other_slot_ref, other_ref, back_ref, out_ref, wide_ref, back_wide, *sums):
    widen(other_ref, wide_ref)
    widen(back_ref, back_wide)
    rows = out_ref.shape[0]
    def clear(first):
        for total in sums:
            total[pl.ds(first, 64)] = jnp.zeros((64, 2, HALF), jnp.float32)
    loop(rows, 64, clear)
    examples = back_ref.shape[0]
    bag = slot_ref.shape[0] // examples
    lanes = len(sums)
    share = examples // lanes
    def body(e):
        backs = [back_wide[lane * share + e] for lane in range(lanes)]
        for l in range(bag):
            for lane, total in enumerate(sums):
                place = (lane * share + e) * bag + l
                row = slot_ref[place]
                total[row] = total[row] + backs[lane] * wide_ref[other_slot_ref[place]]
    loop(share, 1, body)
    def finish(first):
        at = pl.ds(first, 64)
        value = joined(sums[0], at)
        for total in sums[1:]:
            value = value + joined(total, at)
        out_ref[at, :] = value.astype(jnp.bfloat16)
    loop(rows, 64, finish)

def spread_rows(slot, other_slot, other, back, rows, lanes):
    features = other.shape[1]
    return pl.pallas_call(
        spread_kernel,
        out_shape=jax.ShapeDtypeStruct((rows, features), jnp.bfloat16),
        in_specs=[whole(pltpu.SMEM), whole(pltpu.SMEM), whole(), whole()],
        out_specs=whole(),
        scratch_shapes=[pltpu.VMEM((other.shape[0], 2, HALF), jnp.float32), pltpu.VMEM((back.shape[0], 2, HALF), jnp.float32)]
        + [pltpu.VMEM((rows, 2, HALF), jnp.float32) for _ in range(lanes)],
        compiler_params=params(),
        cost_estimate=cost(38), name="spread_rows")(slot, other_slot, other, back)

def absorb_kernel(steps, batch, index_ref, received_ref, out_ref, total_ref, wide_ref):
    chunk = pl.program_id(0)
    held = total_ref.shape[0]
    @pl.when(chunk == 0)
    def _():
        def clear(first):
            total_ref[pl.ds(first, 64)] = jnp.zeros((64, 2, HALF), jnp.float32)
        loop(held, 64, clear)
    @pl.when(chunk < steps)
    def _():
        widen(received_ref, wide_ref)
        rows = received_ref.shape[0]
        def body(first):
            places = [index_ref[chunk * rows + first + j] for j in range(batch)]
            values = [total_ref[places[j]] + wide_ref[first + j] for j in range(batch)]
            for j in reversed(range(batch)):
                total_ref[places[j]] = values[j]
        loop(rows, batch, body)
    @pl.when(chunk >= steps)
    def _():
        base = (chunk - steps) * out_ref.shape[0]
        def finish(first):
            out_ref[pl.ds(first, 64), :] = joined(total_ref, pl.ds(pl.multiple_of(base + first, 64), 64))
        loop(out_ref.shape[0], 64, finish)

def absorb_rows(index, received, held, batch=16):
    count, features = received.shape
    chunk, steps, block = 1280, count // 1280, 1024
    return pl.pallas_call(
        functools.partial(absorb_kernel, steps, batch),
        grid=(steps + held // block,),
        out_shape=jax.ShapeDtypeStruct((held, features), jnp.float32),
        in_specs=[whole(pltpu.SMEM), pl.BlockSpec((chunk, features), lambda i: (jnp.minimum(i, steps - 1), 0))],
        out_specs=pl.BlockSpec((block, features), lambda i: (jnp.maximum(i - steps, 0), 0)),
        scratch_shapes=[pltpu.VMEM((held, 2, HALF), jnp.float32), pltpu.VMEM((chunk, 2, HALF), jnp.float32)],
        compiler_params=params(),
        cost_estimate=cost(36), name="absorb_rows")(index, received)


def local(
    quotient,
    remainder,
    request_q,
    request_r,
    query_q,
    query_r,
    item_q,
    item_r,
    positive,
    query_w1,
    query_w2,
    query_w3,
    item_w1,
    item_w2,
    item_w3,
):
    features = quotient.shape[1]
    capacity_q = request_q.shape[2]
    examples = query_q.shape[0]
    lists = request_q.shape[1]
    capacity = capacity_q + request_r.shape[2]
    group = lists // lax.axis_size("grp")
    asked = exchange(
        jnp.concatenate(
            [request_q[0], request_r[0], jnp.broadcast_to(positive[None, :], (lists, examples))],
            axis=1,
        )
    )
    asked_q = jnp.maximum(asked[:, :capacity_q], 0).reshape(-1)
    asked_r = asked[:, capacity_q:capacity].reshape(-1)
    positive_all = lax.dynamic_slice_in_dim(
        asked[:, capacity:], lax.axis_index("grp") * group, group, 0
    ).reshape(1, -1)
    shard_r = remainder.shape[0]
    named_r = (asked_r[:, None] == jnp.arange(shard_r, dtype=jnp.int32)[None, :]).astype(
        jnp.bfloat16
    )
    served_r = jnp.dot(named_r, remainder, preferred_element_type=jnp.float32).astype(jnp.bfloat16)
    served_q = pick_rows(asked_q, quotient)
    table_r = exchange(served_r.reshape(lists, -1, features)).reshape(-1, features)
    table_q = exchange(served_q.reshape(lists, -1, features)).reshape(-1, features)

    slots_iq, slots_ir = item_q.reshape(-1), item_r.reshape(-1)
    slots_qq, slots_qr = query_q.reshape(-1), query_r.reshape(-1)
    slots_q = jnp.concatenate([slots_qq, slots_iq])
    slots_r = jnp.concatenate([slots_qr, slots_ir])
    pooled = pool_rows(slots_q, slots_r, table_q, table_r, 2 * examples)
    pooled_query, pooled_item = pooled[:examples], pooled[examples:]
    query_unit, query_saved = tower_forward(pooled_query, query_w1, query_w2, query_w3)
    item_unit, item_saved = tower_forward(pooled_item, item_w1, item_w2, item_w3)
    units = jnp.concatenate([item_unit, query_unit], axis=1)
    units_all = gather_group(units)
    items_all, queries_all = units_all[:, :features], units_all[:, features:]

    columns = jnp.arange(items_all.shape[0], dtype=jnp.int32)[None, :]
    weights = score_weights(query_unit, items_all)
    inverse = 1.0 / jnp.sum(weights, axis=1, keepdims=True)
    target = (positive[:, None] == columns).astype(jnp.float32)
    d_query = SCALE * jnp.dot(
        (weights * inverse - target).astype(jnp.bfloat16),
        items_all,
        preferred_element_type=jnp.float32,
    )
    inverse_all = lax.all_to_all(
        jnp.broadcast_to(inverse[:, 0][None, :], (group, examples)),
        GROUP_AXES,
        split_axis=0,
        concat_axis=0,
        tiled=True,
    ).reshape(1, -1)
    query_grads, query_back = tower_backward(
        d_query, query_saved, pooled_query, query_w1, query_w2, query_w3
    )
    own = lax.axis_index(GROUP_AXES) * examples + jnp.arange(examples, dtype=jnp.int32)
    weights_t = score_weights(item_unit, queries_all)
    target_t = (positive_all == own[:, None]).astype(jnp.float32)
    d_item = SCALE * jnp.dot(
        (weights_t * inverse_all - target_t).astype(jnp.bfloat16),
        queries_all,
        preferred_element_type=jnp.float32,
    )
    query_terms = core_sum(query_grads)
    d_item, query_terms = lax.optimization_barrier((d_item, query_terms))
    item_grads, item_back = tower_backward(
        d_item, item_saved, pooled_item, item_w1, item_w2, item_w3
    )
    item_terms = core_sum(item_grads)
    back_all = jnp.concatenate([query_back, item_back], axis=0)
    terms = jnp.concatenate([query_terms, item_terms], axis=2)
    back_all, terms = lax.optimization_barrier((back_all, terms))
    part = chip_sum(terms)
    sums_q = spread_rows(slots_q, slots_r, table_r, back_all, table_q.shape[0], 2)
    sums_q, part = lax.optimization_barrier((sums_q, part))
    summed = lax.all_gather(part, ("core", "grp", "chip"), axis=0, tiled=True)
    back_q = exchange(sums_q.reshape(lists, -1, features)).reshape(-1, features)
    sums_r = spread_rows(slots_r, slots_q, table_q, back_all, table_r.shape[0], 4)
    back_q, sums_r = lax.optimization_barrier((back_q, sums_r))
    back_r = exchange(sums_r.reshape(lists, -1, features)).reshape(-1, features)
    hidden = query_w2.shape[0]
    weights_out = []
    for both in jnp.split(summed, 2, axis=1):
        second, third, first_t = jnp.split(both, [hidden, hidden + features], axis=1)
        weights_out += [first_t.T, second, third]
    asked_q, *weights_out = lax.optimization_barrier((asked_q, *weights_out))
    grad_quotient = absorb_rows(asked_q, back_q, quotient.shape[0])
    grad_quotient, back_r = lax.optimization_barrier((grad_quotient, back_r))
    grad_remainder = inner(named_r, back_r)
    return (grad_quotient, grad_remainder, *weights_out)


def solution(mesh):
    groups, members = mesh.devices.shape
    cores = Mesh(mesh.devices.reshape(groups, members // 2, 2), MESH_AXES)
    rows = P(MESH_AXES)
    return jax.shard_map(
        local,
        mesh=cores,
        in_specs=(rows,) * 9 + (P(),) * 6,
        out_specs=(rows,) * 2 + (P(),) * 6,
        check_vma=False,
    )
```

```python
import functools

import jax
import jax.numpy as jnp
from jax import lax
from jax.experimental import pallas as pl
from jax.experimental.pallas import tpu as pltpu
from jax.sharding import Mesh
from jax.sharding import PartitionSpec as P

SCALE = 20.0
EPS = 1e-06
GROUP_AXES = ("chip", "core")
MESH_AXES = ("grp", "chip", "core")
VMEM_LIMIT = 60 * 1024 * 1024
HALF = 128


def inner(left, right):
    return lax.dot_general(
        left, right, (((0,), (0,)), ((), ())), preferred_element_type=jnp.float32
    )


def outer_t(left, right):
    return lax.dot_general(
        left, right, (((1,), (1,)), ((), ())), preferred_element_type=jnp.float32
    )


def gelu_back(pre_value, upstream):
    return jax.vjp(jax.nn.gelu, pre_value)[1](upstream)[0]


def tower_forward(pooled, first, second, third):
    pre_one = jnp.dot(pooled, first, preferred_element_type=jnp.float32)
    act_one = jax.nn.gelu(pre_one).astype(jnp.bfloat16)
    pre_two = jnp.dot(act_one, second, preferred_element_type=jnp.float32)
    act_two = jax.nn.gelu(pre_two).astype(jnp.bfloat16)
    vector = jnp.dot(act_two, third, preferred_element_type=jnp.float32)
    inv_norm = lax.rsqrt(jnp.sum(vector * vector, axis=1, keepdims=True) + EPS)
    unit_vec = (vector * inv_norm).astype(jnp.bfloat16)
    return (unit_vec, (pre_one, act_one, pre_two, act_two, vector, inv_norm))


def tower_backward(d_unit, saved, pooled, first, second, third):
    pre_one, act_one, pre_two, act_two, vector, inv_norm = saved
    along = jnp.sum(vector * d_unit, axis=1, keepdims=True)
    cubed = inv_norm * inv_norm * inv_norm
    d_vector = (inv_norm * d_unit - cubed * vector * along).astype(jnp.bfloat16)
    grad_third = inner(act_two, d_vector)
    d_pre_two = gelu_back(pre_two, outer_t(d_vector, third)).astype(jnp.bfloat16)
    grad_second = inner(act_one, d_pre_two)
    d_pre_one = gelu_back(pre_one, outer_t(d_pre_two, second)).astype(jnp.bfloat16)
    grad_first_t = inner(d_pre_one, pooled)
    d_pooled = outer_t(d_pre_one, first)
    grads = jnp.concatenate([grad_second, grad_third, grad_first_t], axis=1)
    return (grads, d_pooled)


def score_weights(left, right):
    return jnp.exp(SCALE * outer_t(left, right) - SCALE)


def gather_group(values):
    return lax.all_gather(values, GROUP_AXES, axis=0, tiled=True)


def exchange(rows):
    return lax.all_to_all(rows, MESH_AXES, split_axis=0, concat_axis=0, tiled=True)


def core_sum(grads):
    core, half = lax.axis_index("core"), grads.shape[0] // 2
    kept = lax.dynamic_slice_in_dim(grads, core * half, half, 0)
    given = lax.dynamic_slice_in_dim(grads, (1 - core) * half, half, 0).astype(jnp.bfloat16)
    got = lax.ppermute(given, "core", [(0, 1), (1, 0)])
    chips = lax.axis_size(("grp", "chip"))
    return (kept + got.astype(jnp.float32)).astype(jnp.bfloat16).reshape(chips, half // chips, -1)


def chip_sum(terms):
    terms = lax.all_to_all(terms, ("grp", "chip"), split_axis=0, concat_axis=0, tiled=True)
    return jnp.sum(terms.astype(jnp.float32), axis=0).astype(jnp.bfloat16)


def cost(microseconds):
    return pl.CostEstimate(flops=0, bytes_accessed=int(microseconds * 3.6e6), transcendentals=0)


def whole(space=pltpu.VMEM):
    return pl.BlockSpec(memory_space=space)


def params():
    return pltpu.CompilerParams(vmem_limit_bytes=VMEM_LIMIT)


def loop(count, step, body):
    def run(i, carry):
        body(pl.multiple_of(i * step, step))
        return carry

    lax.fori_loop(0, count // step, run, 0)


def row(place):
    return pl.ds(pl.multiple_of(place, 2), 2)


def halves(first, rows):
    place = pl.multiple_of(2 * first, 16)
    return pl.ds(place, rows, stride=2), pl.ds(place + 1, rows, stride=2)


def widen(narrow_ref, wide_ref, step=64):
    def body(first):
        value = narrow_ref[pl.ds(first, step), :].astype(jnp.float32)
        left, right = halves(first, step)
        wide_ref[left, :] = value[:, :HALF]
        wide_ref[right, :] = value[:, HALF:]

    loop(narrow_ref.shape[0], step, body)


def joined(wide_ref, first, rows):
    left, right = halves(first, rows)
    return jnp.concatenate([wide_ref[left, :], wide_ref[right, :]], axis=1)


def clear(*refs):
    def body(first):
        for ref in refs:
            ref[pl.ds(first, 128), :] = jnp.zeros((128, HALF), jnp.float32)

    loop(refs[0].shape[0], 128, body)


def pick_kernel(place_ref, table_ref, out_ref, wide_ref, stage_ref):
    rows = out_ref.shape[0]
    group = stage_ref.shape[0] // 2
    chunk = pl.program_id(0)

    @pl.when(chunk == 0)
    def _():
        widen(table_ref, wide_ref)

    def body(first):
        places = place_ref.at[pl.ds(chunk * rows + first, group)]
        for j in range(group):
            stage_ref[pl.ds(2 * j, 2), :] = wide_ref[row(places[j]), :]
        out_ref[pl.ds(first, group), :] = joined(stage_ref, 0, group).astype(jnp.bfloat16)

    loop(rows, group, body)


def pick_rows(index, table, chunk=2048, group=64):
    count, (held, features) = index.shape[0], table.shape
    return pl.pallas_call(
        pick_kernel,
        grid=(count // chunk,),
        out_shape=jax.ShapeDtypeStruct((count, features), jnp.bfloat16),
        in_specs=[whole(pltpu.SMEM), whole()],
        out_specs=pl.BlockSpec((chunk, features), lambda i: (i, 0)),
        scratch_shapes=[
            pltpu.VMEM((2 * held, HALF), jnp.float32),
            pltpu.VMEM((2 * group, HALF), jnp.float32),
        ],
        compiler_params=params(),
        cost_estimate=cost(12),
        name="pick_rows",
    )(2 * index, table)


def pool_kernel(place_q_ref, place_r_ref, table_q_ref, table_r_ref, out_ref, wide_q, wide_r, stage_ref):
    widen(table_r_ref, wide_r)
    widen(table_q_ref, wide_q)
    examples = out_ref.shape[0]
    bag = place_q_ref.shape[0] // examples
    group = stage_ref.shape[0] // 2

    def body(first):
        for j in range(group):
            bag_at = pl.ds((first + j) * bag, bag)
            places_q, places_r = place_q_ref.at[bag_at], place_r_ref.at[bag_at]
            terms = [
                wide_q[row(places_q[l]), :] * wide_r[row(places_r[l]), :] for l in range(bag)
            ]
            while len(terms) > 1:
                terms = [a + b for a, b in zip(terms[::2], terms[1::2], strict=True)]
            stage_ref[pl.ds(2 * j, 2), :] = terms[0]
        out_ref[pl.ds(first, group), :] = joined(stage_ref, 0, group).astype(jnp.bfloat16)

    loop(examples, group, body)


def pool_rows(slot_q, slot_r, table_q, table_r, examples, group=16):
    features = table_q.shape[1]
    return pl.pallas_call(
        pool_kernel,
        out_shape=jax.ShapeDtypeStruct((examples, features), jnp.bfloat16),
        in_specs=[whole(pltpu.SMEM), whole(pltpu.SMEM), whole(), whole()],
        out_specs=whole(),
        scratch_shapes=[
            pltpu.VMEM((2 * table_q.shape[0], HALF), jnp.float32),
            pltpu.VMEM((2 * table_r.shape[0], HALF), jnp.float32),
            pltpu.VMEM((2 * group, HALF), jnp.float32),
        ],
        compiler_params=params(),
        cost_estimate=cost(18),
        name="pool_rows",
    )(2 * slot_q, 2 * slot_r, table_q, table_r)


def spread_kernel(place_ref, other_place_ref, other_ref, back_ref, out_ref, wide_ref, back_wide, *totals):
    widen(other_ref, wide_ref)
    widen(back_ref, back_wide)
    clear(*totals)
    examples = back_ref.shape[0]
    bag = place_ref.shape[0] // examples
    share = examples // len(totals)

    def body(e):
        lanes = []
        for lane, total in enumerate(totals):
            example = lane * share + e
            bag_at = pl.ds(example * bag, bag)
            back = back_wide[row(2 * example), :]
            lanes.append((total, back, place_ref.at[bag_at], other_place_ref.at[bag_at]))
        for l in range(bag):
            for total, back, places, other_places in lanes:
                at = row(places[l])
                total[at, :] = total[at, :] + back * wide_ref[row(other_places[l]), :]

    loop(share, 1, body)

    def finish(first):
        value = joined(totals[0], first, 64)
        for total in totals[1:]:
            value = value + joined(total, first, 64)
        out_ref[pl.ds(first, 64), :] = value.astype(jnp.bfloat16)

    loop(out_ref.shape[0], 64, finish)


def spread_rows(slot, other_slot, other, back, rows, lanes=4):
    features = other.shape[1]
    return pl.pallas_call(
        spread_kernel,
        out_shape=jax.ShapeDtypeStruct((rows, features), jnp.bfloat16),
        in_specs=[whole(pltpu.SMEM), whole(pltpu.SMEM), whole(), whole()],
        out_specs=whole(),
        scratch_shapes=[
            pltpu.VMEM((2 * other.shape[0], HALF), jnp.float32),
            pltpu.VMEM((2 * back.shape[0], HALF), jnp.float32),
        ]
        + [pltpu.VMEM((2 * rows, HALF), jnp.float32)] * lanes,
        compiler_params=params(),
        cost_estimate=cost(25),
        name="spread_rows",
    )(2 * slot, 2 * other_slot, other, back)


def absorb_kernel(steps, batch, unroll, place_ref, received_ref, out_ref, total_ref, wide_ref):
    chunk = pl.program_id(0)

    @pl.when(chunk == 0)
    def _():
        clear(total_ref)

    @pl.when(chunk < steps)
    def _():
        widen(received_ref, wide_ref)
        rows = received_ref.shape[0]

        def body(first):
            for start in range(0, unroll, batch):
                places = place_ref.at[pl.ds(chunk * rows + first + start, batch)]
                at = [row(places[j]) for j in range(batch)]
                values = [
                    total_ref[at[j], :] + wide_ref[row(2 * (first + start + j)), :]
                    for j in range(batch)
                ]
                for j in reversed(range(batch)):
                    total_ref[at[j], :] = values[j]

        loop(rows, unroll, body)

    @pl.when(chunk >= steps)
    def _():
        base = pl.multiple_of((chunk - steps) * out_ref.shape[0], out_ref.shape[0])

        def finish(first):
            out_ref[pl.ds(first, 64), :] = joined(total_ref, base + first, 64)

        loop(out_ref.shape[0], 64, finish)


def absorb_rows(index, received, held, batch=16, unroll=80):
    count, features = received.shape
    chunk, block = 2560, 2048
    steps = count // chunk
    return pl.pallas_call(
        functools.partial(absorb_kernel, steps, batch, unroll),
        grid=(steps + held // block,),
        out_shape=jax.ShapeDtypeStruct((held, features), jnp.float32),
        in_specs=[
            whole(pltpu.SMEM),
            pl.BlockSpec((chunk, features), lambda i: (jnp.minimum(i, steps - 1), 0)),
        ],
        out_specs=pl.BlockSpec((block, features), lambda i: (jnp.maximum(i - steps, 0), 0)),
        scratch_shapes=[
            pltpu.VMEM((2 * held, HALF), jnp.float32),
            pltpu.VMEM((2 * chunk, HALF), jnp.float32),
        ],
        compiler_params=params(),
        cost_estimate=cost(22),
        name="absorb_rows",
    )(2 * index, received)


def local(
    quotient,
    remainder,
    request_q,
    request_r,
    query_q,
    query_r,
    item_q,
    item_r,
    positive,
    query_w1,
    query_w2,
    query_w3,
    item_w1,
    item_w2,
    item_w3,
):
    features = quotient.shape[1]
    capacity_q = request_q.shape[2]
    examples = query_q.shape[0]
    lists = request_q.shape[1]
    capacity = capacity_q + request_r.shape[2]
    group = lists // lax.axis_size("grp")
    asked = exchange(
        jnp.concatenate(
            [request_q[0], request_r[0], jnp.broadcast_to(positive[None, :], (lists, examples))],
            axis=1,
        )
    )
    asked_q = jnp.maximum(asked[:, :capacity_q], 0).reshape(-1)
    asked_r = asked[:, capacity_q:capacity].reshape(-1)
    positive_all = lax.dynamic_slice_in_dim(
        asked[:, capacity:], lax.axis_index("grp") * group, group, 0
    ).reshape(1, -1)
    shard_r = remainder.shape[0]
    named_r = (asked_r[:, None] == jnp.arange(shard_r, dtype=jnp.int32)[None, :]).astype(
        jnp.bfloat16
    )
    served_r = jnp.dot(named_r, remainder, preferred_element_type=jnp.float32).astype(jnp.bfloat16)
    served_q = pick_rows(asked_q, quotient)
    table_r = exchange(served_r.reshape(lists, -1, features)).reshape(-1, features)
    table_q = exchange(served_q.reshape(lists, -1, features)).reshape(-1, features)

    slots_iq, slots_ir = item_q.reshape(-1), item_r.reshape(-1)
    slots_qq, slots_qr = query_q.reshape(-1), query_r.reshape(-1)
    slots_q = jnp.concatenate([slots_qq, slots_iq])
    slots_r = jnp.concatenate([slots_qr, slots_ir])
    pooled = pool_rows(slots_q, slots_r, table_q, table_r, 2 * examples)
    pooled_query, pooled_item = pooled[:examples], pooled[examples:]
    query_unit, query_saved = tower_forward(pooled_query, query_w1, query_w2, query_w3)
    item_unit, item_saved = tower_forward(pooled_item, item_w1, item_w2, item_w3)
    units = jnp.concatenate([item_unit, query_unit], axis=1)
    units_all = gather_group(units)
    items_all, queries_all = units_all[:, :features], units_all[:, features:]

    columns = jnp.arange(items_all.shape[0], dtype=jnp.int32)[None, :]
    weights = score_weights(query_unit, items_all)
    inverse = 1.0 / jnp.sum(weights, axis=1, keepdims=True)
    target = (positive[:, None] == columns).astype(jnp.float32)
    d_query = SCALE * jnp.dot(
        (weights * inverse - target).astype(jnp.bfloat16),
        items_all,
        preferred_element_type=jnp.float32,
    )
    inverse_all = lax.all_to_all(
        jnp.broadcast_to(inverse[:, 0][None, :], (group, examples)),
        GROUP_AXES,
        split_axis=0,
        concat_axis=0,
        tiled=True,
    ).reshape(1, -1)
    query_grads, query_back = tower_backward(
        d_query, query_saved, pooled_query, query_w1, query_w2, query_w3
    )
    own = lax.axis_index(GROUP_AXES) * examples + jnp.arange(examples, dtype=jnp.int32)
    weights_t = score_weights(item_unit, queries_all)
    target_t = (positive_all == own[:, None]).astype(jnp.float32)
    d_item = SCALE * jnp.dot(
        (weights_t * inverse_all - target_t).astype(jnp.bfloat16),
        queries_all,
        preferred_element_type=jnp.float32,
    )
    query_terms = core_sum(query_grads)
    d_item, query_terms = lax.optimization_barrier((d_item, query_terms))
    query_part = chip_sum(query_terms)
    item_grads, item_back = tower_backward(
        d_item, item_saved, pooled_item, item_w1, item_w2, item_w3
    )
    item_grads, query_part = lax.optimization_barrier((item_grads, query_part))
    item_terms = core_sum(item_grads)
    back_all = jnp.concatenate([query_back, item_back], axis=0)
    back_all, item_terms = lax.optimization_barrier((back_all, item_terms))
    item_part = chip_sum(item_terms)
    sums_q = spread_rows(slots_q, slots_r, table_r, back_all, table_q.shape[0])
    sums_q, item_part = lax.optimization_barrier((sums_q, item_part))
    part = jnp.concatenate([query_part, item_part], axis=1)
    summed = lax.all_gather(part, ("core", "grp", "chip"), axis=0, tiled=True)
    back_q = exchange(sums_q.reshape(lists, -1, features)).reshape(-1, features)
    sums_r = spread_rows(slots_r, slots_q, table_q, back_all, table_r.shape[0])
    back_q, sums_r = lax.optimization_barrier((back_q, sums_r))
    back_r = exchange(sums_r.reshape(lists, -1, features)).reshape(-1, features)
    grad_quotient = absorb_rows(asked_q, back_q, quotient.shape[0])
    grad_quotient, back_r, summed = lax.optimization_barrier((grad_quotient, back_r, summed))
    grad_remainder = inner(named_r, back_r)
    hidden = query_w2.shape[0]
    weights_out = []
    for both in jnp.split(summed, 2, axis=1):
        second, third, first_t = jnp.split(both, [hidden, hidden + features], axis=1)
        weights_out += [first_t.T, second, third]
    return (grad_quotient, grad_remainder, *weights_out)


def solution(mesh):
    groups, members = mesh.devices.shape
    cores = Mesh(mesh.devices.reshape(groups, members // 2, 2), MESH_AXES)
    rows = P(MESH_AXES)
    return jax.shard_map(
        local,
        mesh=cores,
        in_specs=(rows,) * 9 + (P(),) * 6,
        out_specs=(rows,) * 2 + (P(),) * 6,
        check_vma=False,
    )
```

```python
import functools

import jax
import jax.numpy as jnp
from jax import lax
from jax.experimental import pallas as pl
from jax.experimental.pallas import tpu as pltpu
from jax.sharding import Mesh
from jax.sharding import PartitionSpec as P

SCALE = 20.0
EPS = 1e-06
GROUP_AXES = ("z", "x", "core")
MESH_AXES = ("grp", "z", "x", "core")
CORES = [(0, 1), (1, 0)]
VMEM_LIMIT = 60 * 1024 * 1024
HALF = 128


def inner(left, right):
    return lax.dot_general(
        left, right, (((0,), (0,)), ((), ())), preferred_element_type=jnp.float32
    )


def outer_t(left, right):
    return lax.dot_general(
        left, right, (((1,), (1,)), ((), ())), preferred_element_type=jnp.float32
    )


def gelu_back(pre_value, upstream):
    return jax.vjp(jax.nn.gelu, pre_value)[1](upstream)[0]


def tower_forward(pooled, first, second, third):
    pre_one = jnp.dot(pooled, first, preferred_element_type=jnp.float32)
    act_one = jax.nn.gelu(pre_one).astype(jnp.bfloat16)
    pre_two = jnp.dot(act_one, second, preferred_element_type=jnp.float32)
    act_two = jax.nn.gelu(pre_two).astype(jnp.bfloat16)
    vector = jnp.dot(act_two, third, preferred_element_type=jnp.float32)
    inv_norm = lax.rsqrt(jnp.sum(vector * vector, axis=1, keepdims=True) + EPS)
    unit_vec = (vector * inv_norm).astype(jnp.bfloat16)
    return (unit_vec, (pre_one, act_one, pre_two, act_two, vector, inv_norm))


def tower_backward(d_unit, saved, first, second, third):
    pre_one, act_one, pre_two, act_two, vector, inv_norm = saved
    along = jnp.sum(vector * d_unit, axis=1, keepdims=True)
    cubed = inv_norm * inv_norm * inv_norm
    d_vector = (inv_norm * d_unit - cubed * vector * along).astype(jnp.bfloat16)
    d_pre_two = gelu_back(pre_two, outer_t(d_vector, third)).astype(jnp.bfloat16)
    d_pre_one = gelu_back(pre_one, outer_t(d_pre_two, second)).astype(jnp.bfloat16)
    return outer_t(d_pre_one, first), (d_pre_one, d_pre_two, d_vector)


def weight_grads(pooled, saved, backs):
    act_one, act_two = saved[1], saved[3]
    d_pre_one, d_pre_two, d_vector = backs
    grads = (inner(act_one, d_pre_two), inner(act_two, d_vector), inner(d_pre_one, pooled))
    return jnp.concatenate([g.astype(jnp.bfloat16) for g in grads], axis=1)


def score_weights(left, right):
    return jnp.exp(SCALE * outer_t(left, right) - SCALE)


def gather_group(values):
    return lax.all_gather(values, GROUP_AXES, axis=0, tiled=True)


def exchange(rows):
    return lax.all_to_all(rows, MESH_AXES, split_axis=0, concat_axis=0, tiled=True)


def place_of(axis):
    return lax.axis_index(axis), lax.axis_size(axis)


def shifted(value, axis, by):
    size = lax.axis_size(axis)
    return lax.ppermute(value, axis, [(i, (i + by) % size) for i in range(size)])


def ring_sum(value, axis):
    me, size = place_of(axis)
    rows = value.shape[0] // size

    def part(k):
        return lax.dynamic_slice_in_dim(value, lax.rem(me + k, size) * rows, rows, 0)

    got = [shifted(part(k), axis, k) for k in range(1, size)]
    total = part(0).astype(jnp.float32)
    for term in got:
        total = total + term.astype(jnp.float32)
    return total.astype(jnp.bfloat16)


def ring_gather(part, axis):
    me, size = place_of(axis)
    rows = part.shape[0]
    value = jnp.concatenate([part] * size, axis=0)
    for k in range(1, size):
        source = lax.rem(me + size - k, size)
        value = lax.dynamic_update_slice_in_dim(value, shifted(part, axis, k), source * rows, 0)
    return value


def sum_over_devices(grads, axes):
    core, half = lax.axis_index("core"), grads.shape[0] // 2
    kept = lax.dynamic_slice_in_dim(grads, core * half, half, 0)
    given = lax.dynamic_slice_in_dim(grads, (1 - core) * half, half, 0)
    got = lax.ppermute(given, "core", CORES)
    value = (kept.astype(jnp.float32) + got.astype(jnp.float32)).astype(jnp.bfloat16)
    for axis in axes:
        value = ring_sum(value, axis)
    for axis in reversed(axes):
        value = ring_gather(value, axis)
    other = lax.ppermute(value, "core", CORES)
    return value, other


def cost(microseconds):
    return pl.CostEstimate(flops=0, bytes_accessed=int(microseconds * 3.6e6), transcendentals=0)


def whole(space=pltpu.VMEM):
    return pl.BlockSpec(memory_space=space)


def params():
    return pltpu.CompilerParams(vmem_limit_bytes=VMEM_LIMIT)


def loop(count, step, body):
    def run(i, carry):
        body(pl.multiple_of(i * step, step))
        return carry

    lax.fori_loop(0, count // step, run, 0)


def row(place):
    return pl.ds(pl.multiple_of(place, 2), 2)


def halves(first, rows):
    place = pl.multiple_of(2 * first, 16)
    return pl.ds(place, rows, stride=2), pl.ds(place + 1, rows, stride=2)


def widen(narrow_ref, wide_ref, step=64):
    def body(first):
        value = narrow_ref[pl.ds(first, step), :].astype(jnp.float32)
        left, right = halves(first, step)
        wide_ref[left, :] = value[:, :HALF]
        wide_ref[right, :] = value[:, HALF:]

    loop(narrow_ref.shape[0], step, body)


def joined(wide_ref, first, rows):
    left, right = halves(first, rows)
    return jnp.concatenate([wide_ref[left, :], wide_ref[right, :]], axis=1)


def clear(*refs):
    def body(first):
        for ref in refs:
            ref[pl.ds(first, 128), :] = jnp.zeros((128, HALF), jnp.float32)

    loop(refs[0].shape[0], 128, body)


def pick_kernel(place_ref, table_ref, out_ref, wide_ref, stage_ref):
    rows = out_ref.shape[0]
    group = stage_ref.shape[0] // 2
    chunk = pl.program_id(0)

    @pl.when(chunk == 0)
    def _():
        widen(table_ref, wide_ref)

    def body(first):
        places = place_ref.at[pl.ds(chunk * rows + first, group)]
        for j in range(group):
            stage_ref[pl.ds(2 * j, 2), :] = wide_ref[row(places[j]), :]
        out_ref[pl.ds(first, group), :] = joined(stage_ref, 0, group).astype(jnp.bfloat16)

    loop(rows, group, body)


def pick_rows(index, table, chunk=2048, group=64):
    count, (held, features) = index.shape[0], table.shape
    return pl.pallas_call(
        pick_kernel,
        grid=(count // chunk,),
        out_shape=jax.ShapeDtypeStruct((count, features), jnp.bfloat16),
        in_specs=[whole(pltpu.SMEM), whole()],
        out_specs=pl.BlockSpec((chunk, features), lambda i: (i, 0)),
        scratch_shapes=[
            pltpu.VMEM((2 * held, HALF), jnp.float32),
            pltpu.VMEM((2 * group, HALF), jnp.float32),
        ],
        compiler_params=params(),
        cost_estimate=cost(12),
        name="pick_rows",
    )(2 * index, table)


def pool_kernel(place_q_ref, place_r_ref, table_q_ref, table_r_ref, out_ref, wide_q, wide_r, stage_ref):
    widen(table_r_ref, wide_r)
    widen(table_q_ref, wide_q)
    examples = out_ref.shape[0]
    bag = place_q_ref.shape[0] // examples
    group = stage_ref.shape[0] // 2

    def body(first):
        for j in range(group):
            bag_at = pl.ds((first + j) * bag, bag)
            places_q, places_r = place_q_ref.at[bag_at], place_r_ref.at[bag_at]
            terms = [
                wide_q[row(places_q[l]), :] * wide_r[row(places_r[l]), :] for l in range(bag)
            ]
            while len(terms) > 1:
                terms = [a + b for a, b in zip(terms[::2], terms[1::2], strict=True)]
            stage_ref[pl.ds(2 * j, 2), :] = terms[0]
        out_ref[pl.ds(first, group), :] = joined(stage_ref, 0, group).astype(jnp.bfloat16)

    loop(examples, group, body)


def pool_rows(slot_q, slot_r, table_q, table_r, examples, group=16):
    features = table_q.shape[1]
    return pl.pallas_call(
        pool_kernel,
        out_shape=jax.ShapeDtypeStruct((examples, features), jnp.bfloat16),
        in_specs=[whole(pltpu.SMEM), whole(pltpu.SMEM), whole(), whole()],
        out_specs=whole(),
        scratch_shapes=[
            pltpu.VMEM((2 * table_q.shape[0], HALF), jnp.float32),
            pltpu.VMEM((2 * table_r.shape[0], HALF), jnp.float32),
            pltpu.VMEM((2 * group, HALF), jnp.float32),
        ],
        compiler_params=params(),
        cost_estimate=cost(18),
        name="pool_rows",
    )(2 * slot_q, 2 * slot_r, table_q, table_r)


def spread_kernel(place_ref, other_place_ref, other_ref, back_ref, out_ref, wide_ref, back_wide, *totals):
    widen(other_ref, wide_ref)
    widen(back_ref, back_wide)
    clear(*totals)
    examples = back_ref.shape[0]
    bag = place_ref.shape[0] // examples
    share = examples // len(totals)

    def body(e):
        lanes = []
        for lane, total in enumerate(totals):
            example = lane * share + e
            bag_at = pl.ds(example * bag, bag)
            back = back_wide[row(2 * example), :]
            lanes.append((total, back, place_ref.at[bag_at], other_place_ref.at[bag_at]))
        for l in range(bag):
            for total, back, places, other_places in lanes:
                at = row(places[l])
                total[at, :] = total[at, :] + back * wide_ref[row(other_places[l]), :]

    loop(share, 1, body)

    def finish(first):
        value = joined(totals[0], first, 64)
        for total in totals[1:]:
            value = value + joined(total, first, 64)
        out_ref[pl.ds(first, 64), :] = value.astype(jnp.bfloat16)

    loop(out_ref.shape[0], 64, finish)


def spread_rows(slot, other_slot, other, back, rows, estimate, lanes=4):
    features = other.shape[1]
    return pl.pallas_call(
        spread_kernel,
        out_shape=jax.ShapeDtypeStruct((rows, features), jnp.bfloat16),
        in_specs=[whole(pltpu.SMEM), whole(pltpu.SMEM), whole(), whole()],
        out_specs=whole(),
        scratch_shapes=[
            pltpu.VMEM((2 * other.shape[0], HALF), jnp.float32),
            pltpu.VMEM((2 * back.shape[0], HALF), jnp.float32),
        ]
        + [pltpu.VMEM((2 * rows, HALF), jnp.float32)] * lanes,
        compiler_params=params(),
        cost_estimate=cost(estimate),
        name="spread_rows",
    )(2 * slot, 2 * other_slot, other, back)


def absorb_kernel(steps, batch, unroll, place_ref, received_ref, out_ref, total_ref, wide_ref):
    chunk = pl.program_id(0)

    @pl.when(chunk == 0)
    def _():
        clear(total_ref)

    @pl.when(chunk < steps)
    def _():
        widen(received_ref, wide_ref)
        rows = received_ref.shape[0]

        def body(first):
            for start in range(0, unroll, batch):
                places = place_ref.at[pl.ds(chunk * rows + first + start, batch)]
                at = [row(places[j]) for j in range(batch)]
                values = [
                    total_ref[at[j], :] + wide_ref[row(2 * (first + start + j)), :]
                    for j in range(batch)
                ]
                for j in reversed(range(batch)):
                    total_ref[at[j], :] = values[j]

        loop(rows, unroll, body)

    @pl.when(chunk >= steps)
    def _():
        base = pl.multiple_of((chunk - steps) * out_ref.shape[0], out_ref.shape[0])

        def finish(first):
            out_ref[pl.ds(first, 64), :] = joined(total_ref, base + first, 64)

        loop(out_ref.shape[0], 64, finish)


def absorb_rows(index, received, held, batch=16, unroll=80):
    count, features = received.shape
    chunk, block = 2560, 2048
    steps = count // chunk
    return pl.pallas_call(
        functools.partial(absorb_kernel, steps, batch, unroll),
        grid=(steps + held // block,),
        out_shape=jax.ShapeDtypeStruct((held, features), jnp.float32),
        in_specs=[
            whole(pltpu.SMEM),
            pl.BlockSpec((chunk, features), lambda i: (jnp.minimum(i, steps - 1), 0)),
        ],
        out_specs=pl.BlockSpec((block, features), lambda i: (jnp.maximum(i - steps, 0), 0)),
        scratch_shapes=[
            pltpu.VMEM((2 * held, HALF), jnp.float32),
            pltpu.VMEM((2 * chunk, HALF), jnp.float32),
        ],
        compiler_params=params(),
        cost_estimate=cost(22),
        name="absorb_rows",
    )(2 * index, received)


def local(
    quotient,
    remainder,
    request_q,
    request_r,
    query_q,
    query_r,
    item_q,
    item_r,
    positive,
    query_w1,
    query_w2,
    query_w3,
    item_w1,
    item_w2,
    item_w3,
):
    features = quotient.shape[1]
    capacity_q = request_q.shape[2]
    examples = query_q.shape[0]
    lists = request_q.shape[1]
    capacity = capacity_q + request_r.shape[2]
    group = lists // lax.axis_size("grp")
    asked = exchange(
        jnp.concatenate(
            [request_q[0], request_r[0], jnp.broadcast_to(positive[None, :], (lists, examples))],
            axis=1,
        )
    )
    asked_q = jnp.maximum(asked[:, :capacity_q], 0).reshape(-1)
    asked_r = asked[:, capacity_q:capacity].reshape(-1)
    positive_all = lax.dynamic_slice_in_dim(
        asked[:, capacity:], lax.axis_index("grp") * group, group, 0
    ).reshape(1, -1)
    shard_r = remainder.shape[0]
    named_r = (asked_r[:, None] == jnp.arange(shard_r, dtype=jnp.int32)[None, :]).astype(
        jnp.bfloat16
    )
    served_r = jnp.dot(named_r, remainder, preferred_element_type=jnp.float32).astype(jnp.bfloat16)
    served_q = pick_rows(asked_q, quotient)
    table_r = exchange(served_r.reshape(lists, -1, features)).reshape(-1, features)
    table_q = exchange(served_q.reshape(lists, -1, features)).reshape(-1, features)

    slots_iq, slots_ir = item_q.reshape(-1), item_r.reshape(-1)
    slots_qq, slots_qr = query_q.reshape(-1), query_r.reshape(-1)
    slots_q = jnp.concatenate([slots_qq, slots_iq])
    slots_r = jnp.concatenate([slots_qr, slots_ir])
    pooled = pool_rows(slots_q, slots_r, table_q, table_r, 2 * examples)
    pooled_query, pooled_item = pooled[:examples], pooled[examples:]
    query_unit, query_saved = tower_forward(pooled_query, query_w1, query_w2, query_w3)
    item_unit, item_saved = tower_forward(pooled_item, item_w1, item_w2, item_w3)
    units = jnp.concatenate([item_unit, query_unit], axis=1)
    units_all = gather_group(units)
    items_all, queries_all = units_all[:, :features], units_all[:, features:]

    columns = jnp.arange(items_all.shape[0], dtype=jnp.int32)[None, :]
    weights = score_weights(query_unit, items_all)
    inverse = 1.0 / jnp.sum(weights, axis=1, keepdims=True)
    target = (positive[:, None] == columns).astype(jnp.float32)
    d_query = SCALE * jnp.dot(
        (weights * inverse - target).astype(jnp.bfloat16),
        items_all,
        preferred_element_type=jnp.float32,
    )
    inverse_all = lax.all_to_all(
        jnp.broadcast_to(inverse[:, 0][None, :], (group, examples)),
        GROUP_AXES,
        split_axis=0,
        concat_axis=0,
        tiled=True,
    ).reshape(1, -1)
    query_back, query_backs = tower_backward(d_query, query_saved, query_w1, query_w2, query_w3)
    own = lax.axis_index(GROUP_AXES) * examples + jnp.arange(examples, dtype=jnp.int32)
    weights_t = score_weights(item_unit, queries_all)
    target_t = (positive_all == own[:, None]).astype(jnp.float32)
    d_item = SCALE * jnp.dot(
        (weights_t * inverse_all - target_t).astype(jnp.bfloat16),
        queries_all,
        preferred_element_type=jnp.float32,
    )
    item_back, item_backs = tower_backward(d_item, item_saved, item_w1, item_w2, item_w3)
    back_all = jnp.concatenate([query_back, item_back], axis=0)
    sums_q = spread_rows(slots_q, slots_r, table_r, back_all, table_q.shape[0], 25)
    sums_q, query_backs, item_backs = lax.optimization_barrier((sums_q, query_backs, item_backs))
    back_q = exchange(sums_q.reshape(lists, -1, features)).reshape(-1, features)
    sums_r = spread_rows(slots_r, slots_q, table_q, back_all, table_r.shape[0], 1)
    query_sum = sum_over_devices(weight_grads(pooled_query, query_saved, query_backs), ("x", "grp", "z"))
    item_sum = sum_over_devices(weight_grads(pooled_item, item_saved, item_backs), ("z", "grp", "x"))
    back_q, sums_r = lax.optimization_barrier((back_q, sums_r))
    back_r = exchange(sums_r.reshape(lists, -1, features)).reshape(-1, features)
    grad_quotient = absorb_rows(asked_q, back_q, quotient.shape[0])
    grad_quotient, back_r = lax.optimization_barrier((grad_quotient, back_r))
    grad_remainder = inner(named_r, back_r)
    hidden = query_w2.shape[0]
    low = lax.axis_index("core") == 0

    def piece(halves_got, start, end):
        value, other = (half[:, start:end] for half in halves_got)
        return jnp.where(
            low, jnp.concatenate([value, other], axis=0), jnp.concatenate([other, value], axis=0)
        )

    weights_out = []
    for got in (query_sum, item_sum):
        weights_out += [
            piece(got, hidden + features, hidden + 2 * features).T,
            piece(got, 0, hidden),
            piece(got, hidden, hidden + features),
        ]
    return (grad_quotient, grad_remainder, *weights_out)


def solution(mesh):
    cores = Mesh(mesh.devices.reshape(4, 4, 4, 2), MESH_AXES)
    rows = P(MESH_AXES)
    return jax.shard_map(
        local,
        mesh=cores,
        in_specs=(rows,) * 9 + (P(),) * 6,
        out_specs=(rows,) * 2 + (P(),) * 6,
        check_vma=False,
    )
```

```python
import functools

import jax
import jax.numpy as jnp
from jax import lax
from jax.experimental import pallas as pl
from jax.experimental.pallas import tpu as pltpu
from jax.sharding import Mesh
from jax.sharding import PartitionSpec as P

SCALE = 20.0
EPS = 1e-06
GROUP_AXES = ("z", "x", "core")
MESH_AXES = ("grp", "z", "x", "core")
CHIP_AXES = ("grp", "z", "x")
CORES = [(0, 1), (1, 0)]
VMEM_LIMIT = 60 * 1024 * 1024
HALF = 128


def inner(left, right):
    return lax.dot_general(
        left, right, (((0,), (0,)), ((), ())), preferred_element_type=jnp.float32
    )


def outer_t(left, right):
    return lax.dot_general(
        left, right, (((1,), (1,)), ((), ())), preferred_element_type=jnp.float32
    )


def gelu_back(pre_value, upstream):
    return jax.vjp(jax.nn.gelu, pre_value)[1](upstream)[0]


def tower_forward(pooled, first, second, third):
    pre_one = jnp.dot(pooled, first, preferred_element_type=jnp.float32)
    act_one = jax.nn.gelu(pre_one).astype(jnp.bfloat16)
    pre_two = jnp.dot(act_one, second, preferred_element_type=jnp.float32)
    act_two = jax.nn.gelu(pre_two).astype(jnp.bfloat16)
    vector = jnp.dot(act_two, third, preferred_element_type=jnp.float32)
    inv_norm = lax.rsqrt(jnp.sum(vector * vector, axis=1, keepdims=True) + EPS)
    unit_vec = (vector * inv_norm).astype(jnp.bfloat16)
    return (unit_vec, (pre_one, act_one, pre_two, act_two, vector, inv_norm))


def tower_backward(d_unit, saved, first, second, third):
    pre_one, act_one, pre_two, act_two, vector, inv_norm = saved
    along = jnp.sum(vector * d_unit, axis=1, keepdims=True)
    cubed = inv_norm * inv_norm * inv_norm
    d_vector = (inv_norm * d_unit - cubed * vector * along).astype(jnp.bfloat16)
    d_pre_two = gelu_back(pre_two, outer_t(d_vector, third)).astype(jnp.bfloat16)
    d_pre_one = gelu_back(pre_one, outer_t(d_pre_two, second)).astype(jnp.bfloat16)
    return outer_t(d_pre_one, first), (d_pre_one, d_pre_two, d_vector)


def weight_grads(pooled, saved, backs):
    act_one, act_two = saved[1], saved[3]
    d_pre_one, d_pre_two, d_vector = backs
    grads = (inner(act_one, d_pre_two), inner(act_two, d_vector), inner(d_pre_one, pooled))
    return jnp.concatenate([g.astype(jnp.bfloat16) for g in grads], axis=1)


def score_weights(left, right):
    return jnp.exp(SCALE * outer_t(left, right) - SCALE)


def gather_group(values):
    return lax.all_gather(values, GROUP_AXES, axis=0, tiled=True)


def exchange(rows):
    return lax.all_to_all(rows, MESH_AXES, split_axis=0, concat_axis=0, tiled=True)


def core_sum(grads):
    core, half = lax.axis_index("core"), grads.shape[0] // 2
    kept = lax.dynamic_slice_in_dim(grads, core * half, half, 0)
    given = lax.dynamic_slice_in_dim(grads, (1 - core) * half, half, 0)
    got = lax.ppermute(given, "core", CORES)
    chips = lax.axis_size(CHIP_AXES)
    both = kept.astype(jnp.float32) + got.astype(jnp.float32)
    return both.astype(jnp.bfloat16).reshape(chips, half // chips, -1)


def chip_sum(terms):
    terms = lax.all_to_all(terms, CHIP_AXES, split_axis=0, concat_axis=0, tiled=True)
    return jnp.sum(terms.astype(jnp.float32), axis=0).astype(jnp.bfloat16)


def gather_rows(part):
    return lax.all_gather(part, ("core", *CHIP_AXES), axis=0, tiled=True)


def cost(microseconds):
    return pl.CostEstimate(flops=0, bytes_accessed=int(microseconds * 3.6e6), transcendentals=0)


def whole(space=pltpu.VMEM):
    return pl.BlockSpec(memory_space=space)


def params():
    return pltpu.CompilerParams(vmem_limit_bytes=VMEM_LIMIT)


def loop(count, step, body):
    def run(i, carry):
        body(pl.multiple_of(i * step, step))
        return carry

    lax.fori_loop(0, count // step, run, 0)


def row(place):
    return pl.ds(pl.multiple_of(place, 2), 2)


def halves(first, rows):
    place = pl.multiple_of(2 * first, 16)
    return pl.ds(place, rows, stride=2), pl.ds(place + 1, rows, stride=2)


def widen(narrow_ref, wide_ref, step=64):
    def body(first):
        value = narrow_ref[pl.ds(first, step), :].astype(jnp.float32)
        left, right = halves(first, step)
        wide_ref[left, :] = value[:, :HALF]
        wide_ref[right, :] = value[:, HALF:]

    loop(narrow_ref.shape[0], step, body)


def joined(wide_ref, first, rows):
    left, right = halves(first, rows)
    return jnp.concatenate([wide_ref[left, :], wide_ref[right, :]], axis=1)


def clear(*refs):
    def body(first):
        for ref in refs:
            ref[pl.ds(first, 128), :] = jnp.zeros((128, HALF), jnp.float32)

    loop(refs[0].shape[0], 128, body)


def pick_kernel(place_ref, table_ref, out_ref, wide_ref, stage_ref):
    rows = out_ref.shape[0]
    group = stage_ref.shape[0] // 2
    chunk = pl.program_id(0)

    @pl.when(chunk == 0)
    def _():
        widen(table_ref, wide_ref)

    def body(first):
        places = place_ref.at[pl.ds(chunk * rows + first, group)]
        for j in range(group):
            stage_ref[pl.ds(2 * j, 2), :] = wide_ref[row(places[j]), :]
        out_ref[pl.ds(first, group), :] = joined(stage_ref, 0, group).astype(jnp.bfloat16)

    loop(rows, group, body)


def pick_rows(index, table, chunk=2048, group=64):
    count, (held, features) = index.shape[0], table.shape
    return pl.pallas_call(
        pick_kernel,
        grid=(count // chunk,),
        out_shape=jax.ShapeDtypeStruct((count, features), jnp.bfloat16),
        in_specs=[whole(pltpu.SMEM), whole()],
        out_specs=pl.BlockSpec((chunk, features), lambda i: (i, 0)),
        scratch_shapes=[
            pltpu.VMEM((2 * held, HALF), jnp.float32),
            pltpu.VMEM((2 * group, HALF), jnp.float32),
        ],
        compiler_params=params(),
        cost_estimate=cost(12),
        name="pick_rows",
    )(2 * index, table)


def pool_kernel(place_q_ref, place_r_ref, table_q_ref, table_r_ref, out_ref, wide_q, wide_r, stage_ref):
    widen(table_r_ref, wide_r)
    widen(table_q_ref, wide_q)
    examples = out_ref.shape[0]
    bag = place_q_ref.shape[0] // examples
    group = stage_ref.shape[0] // 2

    def body(first):
        for j in range(group):
            bag_at = pl.ds((first + j) * bag, bag)
            places_q, places_r = place_q_ref.at[bag_at], place_r_ref.at[bag_at]
            terms = [
                wide_q[row(places_q[l]), :] * wide_r[row(places_r[l]), :] for l in range(bag)
            ]
            while len(terms) > 1:
                terms = [a + b for a, b in zip(terms[::2], terms[1::2], strict=True)]
            stage_ref[pl.ds(2 * j, 2), :] = terms[0]
        out_ref[pl.ds(first, group), :] = joined(stage_ref, 0, group).astype(jnp.bfloat16)

    loop(examples, group, body)


def pool_rows(slot_q, slot_r, table_q, table_r, examples, group=16):
    features = table_q.shape[1]
    return pl.pallas_call(
        pool_kernel,
        out_shape=jax.ShapeDtypeStruct((examples, features), jnp.bfloat16),
        in_specs=[whole(pltpu.SMEM), whole(pltpu.SMEM), whole(), whole()],
        out_specs=whole(),
        scratch_shapes=[
            pltpu.VMEM((2 * table_q.shape[0], HALF), jnp.float32),
            pltpu.VMEM((2 * table_r.shape[0], HALF), jnp.float32),
            pltpu.VMEM((2 * group, HALF), jnp.float32),
        ],
        compiler_params=params(),
        cost_estimate=cost(18),
        name="pool_rows",
    )(2 * slot_q, 2 * slot_r, table_q, table_r)


def spread_kernel(place_ref, other_place_ref, other_ref, back_ref, out_ref, wide_ref, back_wide, *totals):
    widen(other_ref, wide_ref)
    widen(back_ref, back_wide)
    clear(*totals)
    examples = back_ref.shape[0]
    bag = place_ref.shape[0] // examples
    share = examples // len(totals)

    def body(e):
        lanes = []
        for lane, total in enumerate(totals):
            example = lane * share + e
            bag_at = pl.ds(example * bag, bag)
            back = back_wide[row(2 * example), :]
            lanes.append((total, back, place_ref.at[bag_at], other_place_ref.at[bag_at]))
        for l in range(bag):
            for total, back, places, other_places in lanes:
                at = row(places[l])
                total[at, :] = total[at, :] + back * wide_ref[row(other_places[l]), :]

    loop(share, 1, body)

    def finish(first):
        value = joined(totals[0], first, 64)
        for total in totals[1:]:
            value = value + joined(total, first, 64)
        out_ref[pl.ds(first, 64), :] = value.astype(jnp.bfloat16)

    loop(out_ref.shape[0], 64, finish)


def spread_rows(slot, other_slot, other, back, rows, estimate, lanes=4):
    features = other.shape[1]
    return pl.pallas_call(
        spread_kernel,
        out_shape=jax.ShapeDtypeStruct((rows, features), jnp.bfloat16),
        in_specs=[whole(pltpu.SMEM), whole(pltpu.SMEM), whole(), whole()],
        out_specs=whole(),
        scratch_shapes=[
            pltpu.VMEM((2 * other.shape[0], HALF), jnp.float32),
            pltpu.VMEM((2 * back.shape[0], HALF), jnp.float32),
        ]
        + [pltpu.VMEM((2 * rows, HALF), jnp.float32)] * lanes,
        compiler_params=params(),
        cost_estimate=cost(estimate),
        name="spread_rows",
    )(2 * slot, 2 * other_slot, other, back)


def absorb_kernel(steps, batch, unroll, place_ref, received_ref, out_ref, total_ref, wide_ref):
    chunk = pl.program_id(0)

    @pl.when(chunk == 0)
    def _():
        clear(total_ref)

    @pl.when(chunk < steps)
    def _():
        widen(received_ref, wide_ref)
        rows = received_ref.shape[0]

        def body(first):
            for start in range(0, unroll, batch):
                places = place_ref.at[pl.ds(chunk * rows + first + start, batch)]
                at = [row(places[j]) for j in range(batch)]
                values = [
                    total_ref[at[j], :] + wide_ref[row(2 * (first + start + j)), :]
                    for j in range(batch)
                ]
                for j in reversed(range(batch)):
                    total_ref[at[j], :] = values[j]

        loop(rows, unroll, body)

    @pl.when(chunk >= steps)
    def _():
        base = pl.multiple_of((chunk - steps) * out_ref.shape[0], out_ref.shape[0])

        def finish(first):
            out_ref[pl.ds(first, 64), :] = joined(total_ref, base + first, 64)

        loop(out_ref.shape[0], 64, finish)


def absorb_rows(index, received, held, batch=16, unroll=80):
    count, features = received.shape
    chunk, block = 2560, 2048
    steps = count // chunk
    return pl.pallas_call(
        functools.partial(absorb_kernel, steps, batch, unroll),
        grid=(steps + held // block,),
        out_shape=jax.ShapeDtypeStruct((held, features), jnp.float32),
        in_specs=[
            whole(pltpu.SMEM),
            pl.BlockSpec((chunk, features), lambda i: (jnp.minimum(i, steps - 1), 0)),
        ],
        out_specs=pl.BlockSpec((block, features), lambda i: (jnp.maximum(i - steps, 0), 0)),
        scratch_shapes=[
            pltpu.VMEM((2 * held, HALF), jnp.float32),
            pltpu.VMEM((2 * chunk, HALF), jnp.float32),
        ],
        compiler_params=params(),
        cost_estimate=cost(22),
        name="absorb_rows",
    )(2 * index, received)


def local(
    quotient,
    remainder,
    request_q,
    request_r,
    query_q,
    query_r,
    item_q,
    item_r,
    positive,
    query_w1,
    query_w2,
    query_w3,
    item_w1,
    item_w2,
    item_w3,
):
    features = quotient.shape[1]
    capacity_q = request_q.shape[2]
    examples = query_q.shape[0]
    lists = request_q.shape[1]
    capacity = capacity_q + request_r.shape[2]
    group = lists // lax.axis_size("grp")
    asked = exchange(
        jnp.concatenate(
            [request_q[0], request_r[0], jnp.broadcast_to(positive[None, :], (lists, examples))],
            axis=1,
        )
    )
    asked_q = jnp.maximum(asked[:, :capacity_q], 0).reshape(-1)
    asked_r = asked[:, capacity_q:capacity].reshape(-1)
    positive_all = lax.dynamic_slice_in_dim(
        asked[:, capacity:], lax.axis_index("grp") * group, group, 0
    ).reshape(1, -1)
    shard_r = remainder.shape[0]
    named_r = (asked_r[:, None] == jnp.arange(shard_r, dtype=jnp.int32)[None, :]).astype(
        jnp.bfloat16
    )
    served_r = jnp.dot(named_r, remainder, preferred_element_type=jnp.float32).astype(jnp.bfloat16)
    served_q = pick_rows(asked_q, quotient)
    table_r = exchange(served_r.reshape(lists, -1, features)).reshape(-1, features)
    table_q = exchange(served_q.reshape(lists, -1, features)).reshape(-1, features)

    slots_iq, slots_ir = item_q.reshape(-1), item_r.reshape(-1)
    slots_qq, slots_qr = query_q.reshape(-1), query_r.reshape(-1)
    slots_q = jnp.concatenate([slots_qq, slots_iq])
    slots_r = jnp.concatenate([slots_qr, slots_ir])
    pooled = pool_rows(slots_q, slots_r, table_q, table_r, 2 * examples)
    pooled_query, pooled_item = pooled[:examples], pooled[examples:]
    query_unit, query_saved = tower_forward(pooled_query, query_w1, query_w2, query_w3)
    item_unit, item_saved = tower_forward(pooled_item, item_w1, item_w2, item_w3)
    units = jnp.concatenate([item_unit, query_unit], axis=1)
    units_all = gather_group(units)
    items_all, queries_all = units_all[:, :features], units_all[:, features:]

    columns = jnp.arange(items_all.shape[0], dtype=jnp.int32)[None, :]
    weights = score_weights(query_unit, items_all)
    inverse = 1.0 / jnp.sum(weights, axis=1, keepdims=True)
    target = (positive[:, None] == columns).astype(jnp.float32)
    d_query = SCALE * jnp.dot(
        (weights * inverse - target).astype(jnp.bfloat16),
        items_all,
        preferred_element_type=jnp.float32,
    )
    inverse_all = lax.all_to_all(
        jnp.broadcast_to(inverse[:, 0][None, :], (group, examples)),
        GROUP_AXES,
        split_axis=0,
        concat_axis=0,
        tiled=True,
    ).reshape(1, -1)
    query_back, query_backs = tower_backward(d_query, query_saved, query_w1, query_w2, query_w3)
    inverse_all, query_backs = lax.optimization_barrier((inverse_all, query_backs))
    query_terms = core_sum(weight_grads(pooled_query, query_saved, query_backs))
    inverse_all, query_terms = lax.optimization_barrier((inverse_all, query_terms))
    query_part = chip_sum(query_terms)
    own = lax.axis_index(GROUP_AXES) * examples + jnp.arange(examples, dtype=jnp.int32)
    weights_t = score_weights(item_unit, queries_all)
    target_t = (positive_all == own[:, None]).astype(jnp.float32)
    d_item = SCALE * jnp.dot(
        (weights_t * inverse_all - target_t).astype(jnp.bfloat16),
        queries_all,
        preferred_element_type=jnp.float32,
    )
    item_back, item_backs = tower_backward(d_item, item_saved, item_w1, item_w2, item_w3)
    item_grads = weight_grads(pooled_item, item_saved, item_backs)
    item_grads, query_part = lax.optimization_barrier((item_grads, query_part))
    query_sum = gather_rows(query_part)
    item_terms = core_sum(item_grads)
    back_all = jnp.concatenate([query_back, item_back], axis=0)
    back_all, item_terms = lax.optimization_barrier((back_all, item_terms))
    item_part = chip_sum(item_terms)
    sums_q = spread_rows(slots_q, slots_r, table_r, back_all, table_q.shape[0], 25)
    sums_q, item_part = lax.optimization_barrier((sums_q, item_part))
    back_q = exchange(sums_q.reshape(lists, -1, features)).reshape(-1, features)
    sums_r = spread_rows(slots_r, slots_q, table_q, back_all, table_r.shape[0], 25)
    item_part, query_sum = lax.optimization_barrier((item_part, query_sum))
    item_sum = gather_rows(item_part)
    back_q, sums_r = lax.optimization_barrier((back_q, sums_r))
    back_r = exchange(sums_r.reshape(lists, -1, features)).reshape(-1, features)
    grad_quotient = absorb_rows(asked_q, back_q, quotient.shape[0])
    grad_quotient, back_r, item_sum = lax.optimization_barrier((grad_quotient, back_r, item_sum))
    grad_remainder = inner(named_r, back_r)
    hidden = query_w2.shape[0]
    weights_out = []
    for summed in (query_sum, item_sum):
        second, third, first_t = jnp.split(summed, [hidden, hidden + features], axis=1)
        weights_out += [first_t.T, second, third]
    return (grad_quotient, grad_remainder, *weights_out)


def solution(mesh):
    cores = Mesh(mesh.devices.reshape(4, 4, 4, 2), MESH_AXES)
    rows = P(MESH_AXES)
    return jax.shard_map(
        local,
        mesh=cores,
        in_specs=(rows,) * 9 + (P(),) * 6,
        out_specs=(rows,) * 2 + (P(),) * 6,
        check_vma=False,
    )
```

```python
import functools

import jax
import jax.numpy as jnp
from jax import lax
from jax.experimental import pallas as pl
from jax.experimental.layout import Layout, with_layout_constraint
from jax.experimental.pallas import tpu as pltpu
from jax.sharding import Mesh
from jax.sharding import PartitionSpec as P

SCALE = 20.0
EPS = 1e-06
GROUP_AXES = ("z", "x", "core")
MESH_AXES = ("grp", "z", "x", "core")
CHIP_AXES = ("grp", "z", "x")
CORES = [(0, 1), (1, 0)]
VMEM_LIMIT = 60 * 1024 * 1024
HALF = 128


def inner(left, right):
    return lax.dot_general(
        left, right, (((0,), (0,)), ((), ())), preferred_element_type=jnp.float32
    )


def outer_t(left, right):
    return lax.dot_general(
        left, right, (((1,), (1,)), ((), ())), preferred_element_type=jnp.float32
    )


def gelu_back(pre_value, upstream):
    return jax.vjp(jax.nn.gelu, pre_value)[1](upstream)[0]


def tower_forward(pooled, first, second, third):
    pre_one = jnp.dot(pooled, first, preferred_element_type=jnp.float32)
    act_one = jax.nn.gelu(pre_one).astype(jnp.bfloat16)
    pre_two = jnp.dot(act_one, second, preferred_element_type=jnp.float32)
    act_two = jax.nn.gelu(pre_two).astype(jnp.bfloat16)
    vector = jnp.dot(act_two, third, preferred_element_type=jnp.float32)
    inv_norm = lax.rsqrt(jnp.sum(vector * vector, axis=1, keepdims=True) + EPS)
    unit_vec = (vector * inv_norm).astype(jnp.bfloat16)
    return (unit_vec, (pre_one, act_one, pre_two, act_two, vector, inv_norm))


def tower_backward(d_unit, saved, first, second, third):
    pre_one, act_one, pre_two, act_two, vector, inv_norm = saved
    along = jnp.sum(vector * d_unit, axis=1, keepdims=True)
    cubed = inv_norm * inv_norm * inv_norm
    d_vector = (inv_norm * d_unit - cubed * vector * along).astype(jnp.bfloat16)
    d_pre_two = gelu_back(pre_two, outer_t(d_vector, third)).astype(jnp.bfloat16)
    d_pre_one = gelu_back(pre_one, outer_t(d_pre_two, second)).astype(jnp.bfloat16)
    return outer_t(d_pre_one, first), (d_pre_one, d_pre_two, d_vector)


def weight_grads(pooled, saved, backs):
    act_one, act_two = saved[1], saved[3]
    d_pre_one, d_pre_two, d_vector = backs
    grads = (inner(act_one, d_pre_two), inner(act_two, d_vector), inner(d_pre_one, pooled))
    joint = jnp.concatenate([g.astype(jnp.bfloat16) for g in grads], axis=1)
    return with_layout_constraint(joint, Layout(major_to_minor=(0, 1)))


def score_weights(left, right):
    return jnp.exp(SCALE * outer_t(left, right) - SCALE)


def gather_group(values):
    return lax.all_gather(values, GROUP_AXES, axis=0, tiled=True)


def exchange(rows):
    return lax.all_to_all(rows, MESH_AXES, split_axis=0, concat_axis=0, tiled=True)


def core_sum(grads):
    core, half = lax.axis_index("core"), grads.shape[0] // 2
    kept = lax.dynamic_slice_in_dim(grads, core * half, half, 0)
    given = lax.dynamic_slice_in_dim(grads, (1 - core) * half, half, 0)
    got = lax.ppermute(given, "core", CORES)
    chips = lax.axis_size(CHIP_AXES)
    both = kept.astype(jnp.float32) + got.astype(jnp.float32)
    return both.astype(jnp.bfloat16).reshape(chips, half // chips, -1)


def chip_sum(terms):
    terms = lax.all_to_all(terms, CHIP_AXES, split_axis=0, concat_axis=0, tiled=True)
    return jnp.sum(terms.astype(jnp.float32), axis=0).astype(jnp.bfloat16)


def gather_rows(part):
    return lax.all_gather(part, ("core", *CHIP_AXES), axis=0, tiled=True)


def cost(microseconds):
    return pl.CostEstimate(flops=0, bytes_accessed=int(microseconds * 3.6e6), transcendentals=0)


def whole(space=pltpu.VMEM):
    return pl.BlockSpec(memory_space=space)


def params():
    return pltpu.CompilerParams(vmem_limit_bytes=VMEM_LIMIT)


def loop(count, step, body):
    def run(i, carry):
        body(pl.multiple_of(i * step, step))
        return carry

    lax.fori_loop(0, count // step, run, 0)


def row(place):
    return pl.ds(pl.multiple_of(place, 2), 2)


def halves(first, rows):
    place = pl.multiple_of(2 * first, 16)
    return pl.ds(place, rows, stride=2), pl.ds(place + 1, rows, stride=2)


def widen(narrow_ref, wide_ref, step=64):
    def body(first):
        value = narrow_ref[pl.ds(first, step), :].astype(jnp.float32)
        left, right = halves(first, step)
        wide_ref[left, :] = value[:, :HALF]
        wide_ref[right, :] = value[:, HALF:]

    loop(narrow_ref.shape[0], step, body)


def joined(wide_ref, first, rows):
    left, right = halves(first, rows)
    return jnp.concatenate([wide_ref[left, :], wide_ref[right, :]], axis=1)


def clear(*refs):
    def body(first):
        for ref in refs:
            ref[pl.ds(first, 128), :] = jnp.zeros((128, HALF), jnp.float32)

    loop(refs[0].shape[0], 128, body)


def pick_kernel(place_ref, table_ref, out_ref, wide_ref, stage_ref):
    rows = out_ref.shape[0]
    group = stage_ref.shape[0] // 2
    chunk = pl.program_id(0)

    @pl.when(chunk == 0)
    def _():
        widen(table_ref, wide_ref)

    def body(first):
        places = place_ref.at[pl.ds(chunk * rows + first, group)]
        for j in range(group):
            stage_ref[pl.ds(2 * j, 2), :] = wide_ref[row(places[j]), :]
        out_ref[pl.ds(first, group), :] = joined(stage_ref, 0, group).astype(jnp.bfloat16)

    loop(rows, group, body)


def pick_rows(index, table, chunk=2048, group=64):
    count, (held, features) = index.shape[0], table.shape
    return pl.pallas_call(
        pick_kernel,
        grid=(count // chunk,),
        out_shape=jax.ShapeDtypeStruct((count, features), jnp.bfloat16),
        in_specs=[whole(pltpu.SMEM), whole()],
        out_specs=pl.BlockSpec((chunk, features), lambda i: (i, 0)),
        scratch_shapes=[
            pltpu.VMEM((2 * held, HALF), jnp.float32),
            pltpu.VMEM((2 * group, HALF), jnp.float32),
        ],
        compiler_params=params(),
        cost_estimate=cost(12),
        name="pick_rows",
    )(2 * index, table)


def pool_kernel(place_q_ref, place_r_ref, table_q_ref, table_r_ref, out_ref, wide_q, wide_r, stage_ref):
    widen(table_r_ref, wide_r)
    widen(table_q_ref, wide_q)
    examples = out_ref.shape[0]
    bag = place_q_ref.shape[0] // examples
    group = stage_ref.shape[0] // 2

    def body(first):
        for j in range(group):
            bag_at = pl.ds((first + j) * bag, bag)
            places_q, places_r = place_q_ref.at[bag_at], place_r_ref.at[bag_at]
            terms = [
                wide_q[row(places_q[l]), :] * wide_r[row(places_r[l]), :] for l in range(bag)
            ]
            while len(terms) > 1:
                terms = [a + b for a, b in zip(terms[::2], terms[1::2], strict=True)]
            stage_ref[pl.ds(2 * j, 2), :] = terms[0]
        out_ref[pl.ds(first, group), :] = joined(stage_ref, 0, group).astype(jnp.bfloat16)

    loop(examples, group, body)


def pool_rows(slot_q, slot_r, table_q, table_r, examples, group=16):
    features = table_q.shape[1]
    return pl.pallas_call(
        pool_kernel,
        out_shape=jax.ShapeDtypeStruct((examples, features), jnp.bfloat16),
        in_specs=[whole(pltpu.SMEM), whole(pltpu.SMEM), whole(), whole()],
        out_specs=whole(),
        scratch_shapes=[
            pltpu.VMEM((2 * table_q.shape[0], HALF), jnp.float32),
            pltpu.VMEM((2 * table_r.shape[0], HALF), jnp.float32),
            pltpu.VMEM((2 * group, HALF), jnp.float32),
        ],
        compiler_params=params(),
        cost_estimate=cost(18),
        name="pool_rows",
    )(2 * slot_q, 2 * slot_r, table_q, table_r)


def spread_kernel(place_ref, other_place_ref, other_ref, back_ref, out_ref, wide_ref, back_wide, *totals):
    widen(other_ref, wide_ref)
    widen(back_ref, back_wide)
    clear(*totals)
    examples = back_ref.shape[0]
    bag = place_ref.shape[0] // examples
    share = examples // len(totals)

    def body(e):
        lanes = []
        for lane, total in enumerate(totals):
            example = lane * share + e
            bag_at = pl.ds(example * bag, bag)
            back = back_wide[row(2 * example), :]
            lanes.append((total, back, place_ref.at[bag_at], other_place_ref.at[bag_at]))
        for l in range(bag):
            for total, back, places, other_places in lanes:
                at = row(places[l])
                total[at, :] = total[at, :] + back * wide_ref[row(other_places[l]), :]

    loop(share, 1, body)

    def finish(first):
        value = joined(totals[0], first, 64)
        for total in totals[1:]:
            value = value + joined(total, first, 64)
        out_ref[pl.ds(first, 64), :] = value.astype(jnp.bfloat16)

    loop(out_ref.shape[0], 64, finish)


def spread_rows(slot, other_slot, other, back, rows, estimate, lanes=4):
    features = other.shape[1]
    return pl.pallas_call(
        spread_kernel,
        out_shape=jax.ShapeDtypeStruct((rows, features), jnp.bfloat16),
        in_specs=[whole(pltpu.SMEM), whole(pltpu.SMEM), whole(), whole()],
        out_specs=whole(),
        scratch_shapes=[
            pltpu.VMEM((2 * other.shape[0], HALF), jnp.float32),
            pltpu.VMEM((2 * back.shape[0], HALF), jnp.float32),
        ]
        + [pltpu.VMEM((2 * rows, HALF), jnp.float32)] * lanes,
        compiler_params=params(),
        cost_estimate=cost(estimate),
        name="spread_rows",
    )(2 * slot, 2 * other_slot, other, back)


def absorb_kernel(steps, batch, unroll, place_ref, received_ref, out_ref, total_ref, wide_ref):
    chunk = pl.program_id(0)

    @pl.when(chunk == 0)
    def _():
        clear(total_ref)

    @pl.when(chunk < steps)
    def _():
        widen(received_ref, wide_ref)
        rows = received_ref.shape[0]

        def body(first):
            for start in range(0, unroll, batch):
                places = place_ref.at[pl.ds(chunk * rows + first + start, batch)]
                at = [row(places[j]) for j in range(batch)]
                values = [
                    total_ref[at[j], :] + wide_ref[row(2 * (first + start + j)), :]
                    for j in range(batch)
                ]
                for j in reversed(range(batch)):
                    total_ref[at[j], :] = values[j]

        loop(rows, unroll, body)

    @pl.when(chunk >= steps)
    def _():
        base = pl.multiple_of((chunk - steps) * out_ref.shape[0], out_ref.shape[0])

        def finish(first):
            out_ref[pl.ds(first, 64), :] = joined(total_ref, base + first, 64)

        loop(out_ref.shape[0], 64, finish)


def absorb_rows(index, received, held, batch=16, unroll=80):
    count, features = received.shape
    chunk, block = 2560, 2048
    steps = count // chunk
    return pl.pallas_call(
        functools.partial(absorb_kernel, steps, batch, unroll),
        grid=(steps + held // block,),
        out_shape=jax.ShapeDtypeStruct((held, features), jnp.float32),
        in_specs=[
            whole(pltpu.SMEM),
            pl.BlockSpec((chunk, features), lambda i: (jnp.minimum(i, steps - 1), 0)),
        ],
        out_specs=pl.BlockSpec((block, features), lambda i: (jnp.maximum(i - steps, 0), 0)),
        scratch_shapes=[
            pltpu.VMEM((2 * held, HALF), jnp.float32),
            pltpu.VMEM((2 * chunk, HALF), jnp.float32),
        ],
        compiler_params=params(),
        cost_estimate=cost(22),
        name="absorb_rows",
    )(2 * index, received)


def local(
    quotient,
    remainder,
    request_q,
    request_r,
    query_q,
    query_r,
    item_q,
    item_r,
    positive,
    query_w1,
    query_w2,
    query_w3,
    item_w1,
    item_w2,
    item_w3,
):
    features = quotient.shape[1]
    capacity_q = request_q.shape[2]
    examples = query_q.shape[0]
    lists = request_q.shape[1]
    group = lists // lax.axis_size("grp")
    asked = exchange(jnp.concatenate([request_q[0], request_r[0]], axis=1))
    asked_q = jnp.maximum(asked[:, :capacity_q], 0).reshape(-1)
    asked_r = asked[:, capacity_q:].reshape(-1)
    shard_r = remainder.shape[0]
    named_r = (asked_r[:, None] == jnp.arange(shard_r, dtype=jnp.int32)[None, :]).astype(
        jnp.bfloat16
    )
    served_r = jnp.dot(named_r, remainder, preferred_element_type=jnp.float32).astype(jnp.bfloat16)
    served_q = pick_rows(asked_q, quotient)
    table_r = exchange(served_r.reshape(lists, -1, features)).reshape(-1, features)
    table_q = exchange(served_q.reshape(lists, -1, features)).reshape(-1, features)

    slots_iq, slots_ir = item_q.reshape(-1), item_r.reshape(-1)
    slots_qq, slots_qr = query_q.reshape(-1), query_r.reshape(-1)
    slots_q = jnp.concatenate([slots_qq, slots_iq])
    slots_r = jnp.concatenate([slots_qr, slots_ir])
    pooled = pool_rows(slots_q, slots_r, table_q, table_r, 2 * examples)
    pooled_query, pooled_item = pooled[:examples], pooled[examples:]
    query_unit, query_saved = tower_forward(pooled_query, query_w1, query_w2, query_w3)
    item_unit, item_saved = tower_forward(pooled_item, item_w1, item_w2, item_w3)
    units = jnp.concatenate([item_unit, query_unit], axis=1)
    units_all = gather_group(units)
    items_all, queries_all = units_all[:, :features], units_all[:, features:]

    columns = jnp.arange(items_all.shape[0], dtype=jnp.int32)[None, :]
    weights = score_weights(query_unit, items_all)
    inverse = 1.0 / jnp.sum(weights, axis=1, keepdims=True)
    target = (positive[:, None] == columns).astype(jnp.float32)
    d_query = SCALE * jnp.dot(
        (weights * inverse - target).astype(jnp.bfloat16),
        items_all,
        preferred_element_type=jnp.float32,
    )
    told = jnp.stack([inverse[:, 0], positive.astype(jnp.float32)])
    told_all = lax.all_to_all(
        jnp.broadcast_to(told[None], (group, *told.shape)),
        GROUP_AXES,
        split_axis=0,
        concat_axis=0,
        tiled=True,
    )
    query_back, query_backs = tower_backward(d_query, query_saved, query_w1, query_w2, query_w3)
    told_all, query_backs = lax.optimization_barrier((told_all, query_backs))
    query_terms = core_sum(weight_grads(pooled_query, query_saved, query_backs))
    inverse_all, positive_all = (told_all[:, i, :].reshape(1, -1) for i in range(2))
    own = lax.axis_index(GROUP_AXES) * examples + jnp.arange(examples, dtype=jnp.int32)
    weights_t = score_weights(item_unit, queries_all)
    target_t = (positive_all == own[:, None].astype(jnp.float32)).astype(jnp.float32)
    d_item = SCALE * jnp.dot(
        (weights_t * inverse_all - target_t).astype(jnp.bfloat16),
        queries_all,
        preferred_element_type=jnp.float32,
    )
    item_back, item_backs = tower_backward(d_item, item_saved, item_w1, item_w2, item_w3)
    item_terms = core_sum(weight_grads(pooled_item, item_saved, item_backs))
    back_all = jnp.concatenate([query_back, item_back], axis=0)
    terms = jnp.concatenate([query_terms, item_terms], axis=2)
    back_all, terms = lax.optimization_barrier((back_all, terms))
    part = chip_sum(terms)
    sums_q = spread_rows(slots_q, slots_r, table_r, back_all, table_q.shape[0], 25)
    sums_r = spread_rows(slots_r, slots_q, table_q, back_all, table_r.shape[0], 25)
    sums_q, sums_r, part = lax.optimization_barrier((sums_q, sums_r, part))
    summed = gather_rows(part)
    back_q = exchange(sums_q.reshape(lists, -1, features)).reshape(-1, features)
    back_q, sums_r = lax.optimization_barrier((back_q, sums_r))
    back_r = exchange(sums_r.reshape(lists, -1, features)).reshape(-1, features)
    grad_quotient = absorb_rows(asked_q, back_q, quotient.shape[0])
    grad_quotient, back_r, summed = lax.optimization_barrier((grad_quotient, back_r, summed))
    grad_remainder = inner(named_r, back_r)
    hidden = query_w2.shape[0]
    weights_out = []
    for both in jnp.split(summed, 2, axis=1):
        second, third, first_t = jnp.split(both, [hidden, hidden + features], axis=1)
        weights_out += [first_t.T, second, third]
    return (grad_quotient, grad_remainder, *weights_out)


def solution(mesh):
    cores = Mesh(mesh.devices.reshape(4, 4, 4, 2), MESH_AXES)
    rows = P(MESH_AXES)
    return jax.shard_map(
        local,
        mesh=cores,
        in_specs=(rows,) * 9 + (P(),) * 6,
        out_specs=(rows,) * 2 + (P(),) * 6,
        check_vma=False,
    )
```

```python
import functools

import jax
import jax.numpy as jnp
from jax import lax
from jax.experimental import pallas as pl
from jax.experimental.layout import Layout, with_layout_constraint
from jax.experimental.pallas import tpu as pltpu
from jax.sharding import Mesh
from jax.sharding import PartitionSpec as P

SCALE = 20.0
EPS = 1e-06
GROUP_AXES = ("z", "x", "core")
MESH_AXES = ("grp", "z", "x", "core")
CHIP_AXES = ("grp", "z", "x")
CORES = [(0, 1), (1, 0)]
VMEM_LIMIT = 60 * 1024 * 1024
HALF = 128


def inner(left, right):
    return lax.dot_general(
        left, right, (((0,), (0,)), ((), ())), preferred_element_type=jnp.float32
    )


def outer_t(left, right):
    return lax.dot_general(
        left, right, (((1,), (1,)), ((), ())), preferred_element_type=jnp.float32
    )


def gelu_back(pre_value, upstream):
    return jax.vjp(jax.nn.gelu, pre_value)[1](upstream)[0]


def tower_forward(pooled, first, second, third):
    pre_one = jnp.dot(pooled, first, preferred_element_type=jnp.float32)
    act_one = jax.nn.gelu(pre_one).astype(jnp.bfloat16)
    pre_two = jnp.dot(act_one, second, preferred_element_type=jnp.float32)
    act_two = jax.nn.gelu(pre_two).astype(jnp.bfloat16)
    vector = jnp.dot(act_two, third, preferred_element_type=jnp.float32)
    inv_norm = lax.rsqrt(jnp.sum(vector * vector, axis=1, keepdims=True) + EPS)
    unit_vec = (vector * inv_norm).astype(jnp.bfloat16)
    return (unit_vec, (pre_one, act_one, pre_two, act_two, vector, inv_norm))


def tower_backward(d_unit, saved, first, second, third):
    pre_one, act_one, pre_two, act_two, vector, inv_norm = saved
    along = jnp.sum(vector * d_unit, axis=1, keepdims=True)
    cubed = inv_norm * inv_norm * inv_norm
    d_vector = (inv_norm * d_unit - cubed * vector * along).astype(jnp.bfloat16)
    d_pre_two = gelu_back(pre_two, outer_t(d_vector, third)).astype(jnp.bfloat16)
    d_pre_one = gelu_back(pre_one, outer_t(d_pre_two, second)).astype(jnp.bfloat16)
    return outer_t(d_pre_one, first), (d_pre_one, d_pre_two, d_vector)


def weight_grads(pooled, saved, backs):
    act_one, act_two = saved[1], saved[3]
    d_pre_one, d_pre_two, d_vector = backs
    grads = (inner(act_one, d_pre_two), inner(act_two, d_vector), inner(d_pre_one, pooled))
    joint = jnp.concatenate([g.astype(jnp.bfloat16) for g in grads], axis=1)
    return with_layout_constraint(joint, Layout(major_to_minor=(0, 1)))


def score_weights(left, right):
    return jnp.exp(SCALE * outer_t(left, right) - SCALE)


def gather_group(values):
    return lax.all_gather(values, GROUP_AXES, axis=0, tiled=True)


def exchange(rows):
    return lax.all_to_all(rows, MESH_AXES, split_axis=0, concat_axis=0, tiled=True)


def core_sum(grads):
    core, half = lax.axis_index("core"), grads.shape[0] // 2
    kept = lax.dynamic_slice_in_dim(grads, core * half, half, 0)
    given = lax.dynamic_slice_in_dim(grads, (1 - core) * half, half, 0)
    got = lax.ppermute(given, "core", CORES)
    chips = lax.axis_size(CHIP_AXES)
    both = kept.astype(jnp.float32) + got.astype(jnp.float32)
    return both.astype(jnp.bfloat16).reshape(chips, half // chips, -1)


def chip_sum(terms):
    terms = lax.all_to_all(terms, CHIP_AXES, split_axis=0, concat_axis=0, tiled=True)
    return jnp.sum(terms.astype(jnp.float32), axis=0).astype(jnp.bfloat16)


def gather_rows(part):
    return lax.all_gather(part, ("core", *CHIP_AXES), axis=0, tiled=True)


def cost(microseconds):
    return pl.CostEstimate(flops=0, bytes_accessed=int(microseconds * 3.6e6), transcendentals=0)


def whole(space=pltpu.VMEM):
    return pl.BlockSpec(memory_space=space)


def params():
    return pltpu.CompilerParams(vmem_limit_bytes=VMEM_LIMIT)


def loop(count, step, body):
    def run(i, carry):
        body(pl.multiple_of(i * step, step))
        return carry

    lax.fori_loop(0, count // step, run, 0)


def row(place):
    return pl.ds(pl.multiple_of(place, 2), 2)


def halves(first, rows):
    place = pl.multiple_of(2 * first, 16)
    return pl.ds(place, rows, stride=2), pl.ds(place + 1, rows, stride=2)


def widen(narrow_ref, wide_ref, step=64):
    def body(first):
        value = narrow_ref[pl.ds(first, step), :].astype(jnp.float32)
        left, right = halves(first, step)
        wide_ref[left, :] = value[:, :HALF]
        wide_ref[right, :] = value[:, HALF:]

    loop(narrow_ref.shape[0], step, body)


def joined(wide_ref, first, rows):
    left, right = halves(first, rows)
    return jnp.concatenate([wide_ref[left, :], wide_ref[right, :]], axis=1)


def clear(*refs):
    def body(first):
        for ref in refs:
            ref[pl.ds(first, 128), :] = jnp.zeros((128, HALF), jnp.float32)

    loop(refs[0].shape[0], 128, body)


def pick_kernel(place_ref, table_ref, out_ref, wide_ref, stage_ref):
    rows = out_ref.shape[0]
    group = stage_ref.shape[0] // 2
    chunk = pl.program_id(0)

    @pl.when(chunk == 0)
    def _():
        widen(table_ref, wide_ref)

    def body(first):
        places = place_ref.at[pl.ds(chunk * rows + first, group)]
        for j in range(group):
            stage_ref[pl.ds(2 * j, 2), :] = wide_ref[row(places[j]), :]
        out_ref[pl.ds(first, group), :] = joined(stage_ref, 0, group).astype(jnp.bfloat16)

    loop(rows, group, body)


def pick_rows(index, table, chunk=2048, group=64):
    count, (held, features) = index.shape[0], table.shape
    return pl.pallas_call(
        pick_kernel,
        grid=(count // chunk,),
        out_shape=jax.ShapeDtypeStruct((count, features), jnp.bfloat16),
        in_specs=[whole(pltpu.SMEM), whole()],
        out_specs=pl.BlockSpec((chunk, features), lambda i: (i, 0)),
        scratch_shapes=[
            pltpu.VMEM((2 * held, HALF), jnp.float32),
            pltpu.VMEM((2 * group, HALF), jnp.float32),
        ],
        compiler_params=params(),
        cost_estimate=cost(12),
        name="pick_rows",
    )(2 * index, table)


def pool_kernel(place_q_ref, place_r_ref, table_q_ref, table_r_ref, out_ref, wide_q, wide_r, stage_ref):
    widen(table_r_ref, wide_r)
    widen(table_q_ref, wide_q)
    examples = out_ref.shape[0]
    bag = place_q_ref.shape[0] // examples
    group = stage_ref.shape[0] // 2

    def body(first):
        for j in range(group):
            bag_at = pl.ds((first + j) * bag, bag)
            places_q, places_r = place_q_ref.at[bag_at], place_r_ref.at[bag_at]
            terms = [
                wide_q[row(places_q[l]), :] * wide_r[row(places_r[l]), :] for l in range(bag)
            ]
            while len(terms) > 1:
                terms = [a + b for a, b in zip(terms[::2], terms[1::2], strict=True)]
            stage_ref[pl.ds(2 * j, 2), :] = terms[0]
        out_ref[pl.ds(first, group), :] = joined(stage_ref, 0, group).astype(jnp.bfloat16)

    loop(examples, group, body)


def pool_rows(slot_q, slot_r, table_q, table_r, examples, group=16):
    features = table_q.shape[1]
    return pl.pallas_call(
        pool_kernel,
        out_shape=jax.ShapeDtypeStruct((examples, features), jnp.bfloat16),
        in_specs=[whole(pltpu.SMEM), whole(pltpu.SMEM), whole(), whole()],
        out_specs=whole(),
        scratch_shapes=[
            pltpu.VMEM((2 * table_q.shape[0], HALF), jnp.float32),
            pltpu.VMEM((2 * table_r.shape[0], HALF), jnp.float32),
            pltpu.VMEM((2 * group, HALF), jnp.float32),
        ],
        compiler_params=params(),
        cost_estimate=cost(18),
        name="pool_rows",
    )(2 * slot_q, 2 * slot_r, table_q, table_r)


def spread_kernel(place_ref, other_place_ref, other_ref, back_ref, out_ref, wide_ref, back_wide, *totals):
    widen(other_ref, wide_ref)
    widen(back_ref, back_wide)
    clear(*totals)
    examples = back_ref.shape[0]
    bag = place_ref.shape[0] // examples
    share = examples // len(totals)

    def body(e):
        lanes = []
        for lane, total in enumerate(totals):
            example = lane * share + e
            bag_at = pl.ds(example * bag, bag)
            back = back_wide[row(2 * example), :]
            lanes.append((total, back, place_ref.at[bag_at], other_place_ref.at[bag_at]))
        for l in range(bag):
            for total, back, places, other_places in lanes:
                at = row(places[l])
                total[at, :] = total[at, :] + back * wide_ref[row(other_places[l]), :]

    loop(share, 1, body)

    def finish(first):
        value = joined(totals[0], first, 64)
        for total in totals[1:]:
            value = value + joined(total, first, 64)
        out_ref[pl.ds(first, 64), :] = value.astype(jnp.bfloat16)

    loop(out_ref.shape[0], 64, finish)


def spread_rows(slot, other_slot, other, back, rows, estimate, lanes=4):
    features = other.shape[1]
    return pl.pallas_call(
        spread_kernel,
        out_shape=jax.ShapeDtypeStruct((rows, features), jnp.bfloat16),
        in_specs=[whole(pltpu.SMEM), whole(pltpu.SMEM), whole(), whole()],
        out_specs=whole(),
        scratch_shapes=[
            pltpu.VMEM((2 * other.shape[0], HALF), jnp.float32),
            pltpu.VMEM((2 * back.shape[0], HALF), jnp.float32),
        ]
        + [pltpu.VMEM((2 * rows, HALF), jnp.float32)] * lanes,
        compiler_params=params(),
        cost_estimate=cost(estimate),
        name="spread_rows",
    )(2 * slot, 2 * other_slot, other, back)


def absorb_kernel(steps, batch, unroll, place_ref, received_ref, out_ref, total_ref, wide_ref):
    chunk = pl.program_id(0)

    @pl.when(chunk == 0)
    def _():
        clear(total_ref)

    @pl.when(chunk < steps)
    def _():
        widen(received_ref, wide_ref)
        rows = received_ref.shape[0]

        def body(first):
            for start in range(0, unroll, batch):
                places = place_ref.at[pl.ds(chunk * rows + first + start, batch)]
                at = [row(places[j]) for j in range(batch)]
                values = [
                    total_ref[at[j], :] + wide_ref[row(2 * (first + start + j)), :]
                    for j in range(batch)
                ]
                for j in reversed(range(batch)):
                    total_ref[at[j], :] = values[j]

        loop(rows, unroll, body)

    @pl.when(chunk >= steps)
    def _():
        base = pl.multiple_of((chunk - steps) * out_ref.shape[0], out_ref.shape[0])

        def finish(first):
            out_ref[pl.ds(first, 64), :] = joined(total_ref, base + first, 64)

        loop(out_ref.shape[0], 64, finish)


def absorb_rows(index, received, held, batch=16, unroll=80):
    count, features = received.shape
    chunk, block = 2560, 2048
    steps = count // chunk
    return pl.pallas_call(
        functools.partial(absorb_kernel, steps, batch, unroll),
        grid=(steps + held // block,),
        out_shape=jax.ShapeDtypeStruct((held, features), jnp.float32),
        in_specs=[
            whole(pltpu.SMEM),
            pl.BlockSpec((chunk, features), lambda i: (jnp.minimum(i, steps - 1), 0)),
        ],
        out_specs=pl.BlockSpec((block, features), lambda i: (jnp.maximum(i - steps, 0), 0)),
        scratch_shapes=[
            pltpu.VMEM((2 * held, HALF), jnp.float32),
            pltpu.VMEM((2 * chunk, HALF), jnp.float32),
        ],
        compiler_params=params(),
        cost_estimate=cost(22),
        name="absorb_rows",
    )(2 * index, received)


def local(
    quotient,
    remainder,
    request_q,
    request_r,
    query_q,
    query_r,
    item_q,
    item_r,
    positive,
    query_w1,
    query_w2,
    query_w3,
    item_w1,
    item_w2,
    item_w3,
):
    features = quotient.shape[1]
    capacity_q = request_q.shape[2]
    examples = query_q.shape[0]
    lists = request_q.shape[1]
    group = lists // lax.axis_size("grp")
    asked = exchange(jnp.concatenate([request_q[0], request_r[0]], axis=1))
    asked_q = jnp.maximum(asked[:, :capacity_q], 0).reshape(-1)
    asked_r = asked[:, capacity_q:].reshape(-1)
    shard_r = remainder.shape[0]
    named_r = (asked_r[:, None] == jnp.arange(shard_r, dtype=jnp.int32)[None, :]).astype(
        jnp.bfloat16
    )
    served_r = jnp.dot(named_r, remainder, preferred_element_type=jnp.float32).astype(jnp.bfloat16)
    served_q = pick_rows(asked_q, quotient)
    table_r = exchange(served_r.reshape(lists, -1, features)).reshape(-1, features)
    table_q = exchange(served_q.reshape(lists, -1, features)).reshape(-1, features)

    slots_iq, slots_ir = item_q.reshape(-1), item_r.reshape(-1)
    slots_qq, slots_qr = query_q.reshape(-1), query_r.reshape(-1)
    slots_q = jnp.concatenate([slots_qq, slots_iq])
    slots_r = jnp.concatenate([slots_qr, slots_ir])
    pooled = pool_rows(slots_q, slots_r, table_q, table_r, 2 * examples)
    pooled_query, pooled_item = pooled[:examples], pooled[examples:]
    query_unit, query_saved = tower_forward(pooled_query, query_w1, query_w2, query_w3)
    item_unit, item_saved = tower_forward(pooled_item, item_w1, item_w2, item_w3)
    units = jnp.concatenate([item_unit, query_unit], axis=1)
    units_all = gather_group(units)
    items_all, queries_all = units_all[:, :features], units_all[:, features:]

    columns = jnp.arange(items_all.shape[0], dtype=jnp.int32)[None, :]
    weights = score_weights(query_unit, items_all)
    inverse = 1.0 / jnp.sum(weights, axis=1, keepdims=True)
    target = (positive[:, None] == columns).astype(jnp.float32)
    d_query = SCALE * jnp.dot(
        (weights * inverse - target).astype(jnp.bfloat16),
        items_all,
        preferred_element_type=jnp.float32,
    )
    told = jnp.stack([inverse[:, 0], positive.astype(jnp.float32)])
    told_all = lax.all_to_all(
        jnp.broadcast_to(told[None], (group, *told.shape)),
        GROUP_AXES,
        split_axis=0,
        concat_axis=0,
        tiled=True,
    )
    query_back, query_backs = tower_backward(d_query, query_saved, query_w1, query_w2, query_w3)
    told_all, query_backs = lax.optimization_barrier((told_all, query_backs))
    query_terms = core_sum(weight_grads(pooled_query, query_saved, query_backs))
    inverse_all, positive_all = (told_all[:, i, :].reshape(1, -1) for i in range(2))
    own = lax.axis_index(GROUP_AXES) * examples + jnp.arange(examples, dtype=jnp.int32)
    weights_t = score_weights(item_unit, queries_all)
    target_t = (positive_all == own[:, None].astype(jnp.float32)).astype(jnp.float32)
    d_item = SCALE * jnp.dot(
        (weights_t * inverse_all - target_t).astype(jnp.bfloat16),
        queries_all,
        preferred_element_type=jnp.float32,
    )
    item_back, item_backs = tower_backward(d_item, item_saved, item_w1, item_w2, item_w3)
    item_terms = core_sum(weight_grads(pooled_item, item_saved, item_backs))
    back_all = jnp.concatenate([query_back, item_back], axis=0)
    terms = jnp.concatenate([query_terms, item_terms], axis=2)
    back_all, terms = lax.optimization_barrier((back_all, terms))
    part = chip_sum(terms)
    sums_q = spread_rows(slots_q, slots_r, table_r, back_all, table_q.shape[0], 25)
    sums_q, back_all, part = lax.optimization_barrier((sums_q, back_all, part))
    summed = gather_rows(part)
    sums_r = spread_rows(slots_r, slots_q, table_q, back_all, table_r.shape[0], 25)
    sums_q, sums_r = lax.optimization_barrier((sums_q, sums_r))
    back_q = exchange(sums_q.reshape(lists, -1, features)).reshape(-1, features)
    back_q, sums_r = lax.optimization_barrier((back_q, sums_r))
    back_r = exchange(sums_r.reshape(lists, -1, features)).reshape(-1, features)
    grad_quotient = absorb_rows(asked_q, back_q, quotient.shape[0])
    grad_quotient, back_r = lax.optimization_barrier((grad_quotient, back_r))
    grad_remainder = inner(named_r, back_r)
    grad_remainder, summed = lax.optimization_barrier((grad_remainder, summed))
    hidden = query_w2.shape[0]
    weights_out = []
    for both in jnp.split(summed, 2, axis=1):
        second, third, first_t = jnp.split(both, [hidden, hidden + features], axis=1)
        weights_out += [first_t.T, second, third]
    return (grad_quotient, grad_remainder, *weights_out)


def solution(mesh):
    cores = Mesh(mesh.devices.reshape(4, 4, 4, 2), MESH_AXES)
    rows = P(MESH_AXES)
    return jax.shard_map(
        local,
        mesh=cores,
        in_specs=(rows,) * 9 + (P(),) * 6,
        out_specs=(rows,) * 2 + (P(),) * 6,
        check_vma=False,
    )
```

```python
import functools

import jax
import jax.numpy as jnp
from jax import lax
from jax.experimental import pallas as pl
from jax.experimental.layout import Layout, with_layout_constraint
from jax.experimental.pallas import tpu as pltpu
from jax.sharding import Mesh
from jax.sharding import PartitionSpec as P

SCALE = 20.0
EPS = 1e-06
GROUP_AXES = ("z", "x", "core")
MESH_AXES = ("grp", "z", "x", "core")
CHIP_AXES = ("grp", "z", "x")
CORES = [(0, 1), (1, 0)]
VMEM_LIMIT = 60 * 1024 * 1024
HALF = 128


def inner(left, right):
    return lax.dot_general(
        left, right, (((0,), (0,)), ((), ())), preferred_element_type=jnp.float32
    )


def outer_t(left, right):
    return lax.dot_general(
        left, right, (((1,), (1,)), ((), ())), preferred_element_type=jnp.float32
    )


def gelu_back(pre_value, upstream):
    return jax.vjp(jax.nn.gelu, pre_value)[1](upstream)[0]


def tower_forward(pooled, first, second, third):
    pre_one = jnp.dot(pooled, first, preferred_element_type=jnp.float32)
    act_one = jax.nn.gelu(pre_one).astype(jnp.bfloat16)
    pre_two = jnp.dot(act_one, second, preferred_element_type=jnp.float32)
    act_two = jax.nn.gelu(pre_two).astype(jnp.bfloat16)
    vector = jnp.dot(act_two, third, preferred_element_type=jnp.float32)
    inv_norm = lax.rsqrt(jnp.sum(vector * vector, axis=1, keepdims=True) + EPS)
    unit_vec = (vector * inv_norm).astype(jnp.bfloat16)
    return (unit_vec, (pre_one, act_one, pre_two, act_two, vector, inv_norm))


def tower_backward(d_unit, saved, first, second, third):
    pre_one, act_one, pre_two, act_two, vector, inv_norm = saved
    along = jnp.sum(vector * d_unit, axis=1, keepdims=True)
    cubed = inv_norm * inv_norm * inv_norm
    d_vector = (inv_norm * d_unit - cubed * vector * along).astype(jnp.bfloat16)
    d_pre_two = gelu_back(pre_two, outer_t(d_vector, third)).astype(jnp.bfloat16)
    d_pre_one = gelu_back(pre_one, outer_t(d_pre_two, second)).astype(jnp.bfloat16)
    return outer_t(d_pre_one, first), (d_pre_one, d_pre_two, d_vector)


def weight_grads(pooled, saved, backs):
    act_one, act_two = saved[1], saved[3]
    d_pre_one, d_pre_two, d_vector = backs
    grads = (inner(act_one, d_pre_two), inner(act_two, d_vector), inner(d_pre_one, pooled))
    joint = jnp.concatenate([g.astype(jnp.bfloat16) for g in grads], axis=1)
    return with_layout_constraint(joint, Layout(major_to_minor=(0, 1)))


def score_weights(left, right):
    return jnp.exp(SCALE * outer_t(left, right) - SCALE)


def gather_group(values):
    return lax.all_gather(values, GROUP_AXES, axis=0, tiled=True)


def exchange(rows):
    return lax.all_to_all(rows, MESH_AXES, split_axis=0, concat_axis=0, tiled=True)


def core_sum(grads):
    core, half = lax.axis_index("core"), grads.shape[0] // 2
    kept = lax.dynamic_slice_in_dim(grads, core * half, half, 0)
    given = lax.dynamic_slice_in_dim(grads, (1 - core) * half, half, 0)
    got = lax.ppermute(given, "core", CORES)
    chips = lax.axis_size(CHIP_AXES)
    both = kept.astype(jnp.float32) + got.astype(jnp.float32)
    return both.astype(jnp.bfloat16).reshape(chips, half // chips, -1)


def chip_sum(terms):
    terms = lax.all_to_all(terms, CHIP_AXES, split_axis=0, concat_axis=0, tiled=True)
    return jnp.sum(terms.astype(jnp.float32), axis=0).astype(jnp.bfloat16)


def gather_rows(part):
    return lax.all_gather(part, ("core", *CHIP_AXES), axis=0, tiled=True)


def cost(microseconds):
    return pl.CostEstimate(flops=0, bytes_accessed=int(microseconds * 3.6e6), transcendentals=0)


def whole(space=pltpu.VMEM):
    return pl.BlockSpec(memory_space=space)


def params():
    return pltpu.CompilerParams(vmem_limit_bytes=VMEM_LIMIT)


def loop(count, step, body):
    def run(i, carry):
        body(pl.multiple_of(i * step, step))
        return carry

    lax.fori_loop(0, count // step, run, 0)


def row(place):
    return pl.ds(pl.multiple_of(place, 2), 2)


def halves(first, rows):
    place = pl.multiple_of(2 * first, 16)
    return pl.ds(place, rows, stride=2), pl.ds(place + 1, rows, stride=2)


def widen(narrow_ref, wide_ref, step=64):
    def body(first):
        value = narrow_ref[pl.ds(first, step), :].astype(jnp.float32)
        left, right = halves(first, step)
        wide_ref[left, :] = value[:, :HALF]
        wide_ref[right, :] = value[:, HALF:]

    loop(narrow_ref.shape[0], step, body)


def joined(wide_ref, first, rows):
    left, right = halves(first, rows)
    return jnp.concatenate([wide_ref[left, :], wide_ref[right, :]], axis=1)


def clear(*refs):
    def body(first):
        for ref in refs:
            ref[pl.ds(first, 128), :] = jnp.zeros((128, HALF), jnp.float32)

    loop(refs[0].shape[0], 128, body)


def pick_kernel(place_ref, table_ref, out_ref, wide_ref, stage_ref):
    rows = out_ref.shape[0]
    group = stage_ref.shape[0] // 2
    chunk = pl.program_id(0)

    @pl.when(chunk == 0)
    def _():
        widen(table_ref, wide_ref)

    def body(first):
        places = place_ref.at[pl.ds(chunk * rows + first, group)]
        for j in range(group):
            stage_ref[pl.ds(2 * j, 2), :] = wide_ref[row(places[j]), :]
        out_ref[pl.ds(first, group), :] = joined(stage_ref, 0, group).astype(jnp.bfloat16)

    loop(rows, group, body)


def pick_rows(index, table, chunk=2048, group=64):
    count, (held, features) = index.shape[0], table.shape
    return pl.pallas_call(
        pick_kernel,
        grid=(count // chunk,),
        out_shape=jax.ShapeDtypeStruct((count, features), jnp.bfloat16),
        in_specs=[whole(pltpu.SMEM), whole()],
        out_specs=pl.BlockSpec((chunk, features), lambda i: (i, 0)),
        scratch_shapes=[
            pltpu.VMEM((2 * held, HALF), jnp.float32),
            pltpu.VMEM((2 * group, HALF), jnp.float32),
        ],
        compiler_params=params(),
        cost_estimate=cost(12),
        name="pick_rows",
    )(2 * index, table)


def pool_kernel(place_q_ref, place_r_ref, table_q_ref, table_r_ref, out_ref, wide_q, wide_r, stage_ref):
    widen(table_r_ref, wide_r)
    widen(table_q_ref, wide_q)
    examples = out_ref.shape[0]
    bag = place_q_ref.shape[0] // examples
    group = stage_ref.shape[0] // 2

    def body(first):
        for j in range(group):
            place = (first + j) * bag
            total = None
            for l in range(bag):
                left = wide_q[row(place_q_ref[place + l]), :]
                term = left * wide_r[row(place_r_ref[place + l]), :]
                total = term if total is None else total + term
            stage_ref[pl.ds(2 * j, 2), :] = total
        out_ref[pl.ds(first, group), :] = joined(stage_ref, 0, group).astype(jnp.bfloat16)

    loop(examples, group, body)


def pool_rows(slot_q, slot_r, table_q, table_r, examples, group=16):
    features = table_q.shape[1]
    return pl.pallas_call(
        pool_kernel,
        out_shape=jax.ShapeDtypeStruct((examples, features), jnp.bfloat16),
        in_specs=[whole(pltpu.SMEM), whole(pltpu.SMEM), whole(), whole()],
        out_specs=whole(),
        scratch_shapes=[
            pltpu.VMEM((2 * table_q.shape[0], HALF), jnp.float32),
            pltpu.VMEM((2 * table_r.shape[0], HALF), jnp.float32),
            pltpu.VMEM((2 * group, HALF), jnp.float32),
        ],
        compiler_params=params(),
        cost_estimate=cost(18),
        name="pool_rows",
    )(2 * slot_q, 2 * slot_r, table_q, table_r)


def spread_kernel(place_ref, other_place_ref, other_ref, back_ref, out_ref, wide_ref, back_wide, *totals):
    widen(other_ref, wide_ref)
    widen(back_ref, back_wide)
    clear(*totals)
    examples = back_ref.shape[0]
    bag = place_ref.shape[0] // examples
    share = examples // len(totals)

    def body(e):
        lanes = []
        for lane, total in enumerate(totals):
            example = lane * share + e
            bag_at = pl.ds(example * bag, bag)
            back = back_wide[row(2 * example), :]
            lanes.append((total, back, place_ref.at[bag_at], other_place_ref.at[bag_at]))
        for l in range(bag):
            for total, back, places, other_places in lanes:
                at = row(places[l])
                total[at, :] = total[at, :] + back * wide_ref[row(other_places[l]), :]

    loop(share, 1, body)

    def finish(first):
        value = joined(totals[0], first, 64)
        for total in totals[1:]:
            value = value + joined(total, first, 64)
        out_ref[pl.ds(first, 64), :] = value.astype(jnp.bfloat16)

    loop(out_ref.shape[0], 64, finish)


def spread_rows(slot, other_slot, other, back, rows, estimate, lanes=4):
    features = other.shape[1]
    return pl.pallas_call(
        spread_kernel,
        out_shape=jax.ShapeDtypeStruct((rows, features), jnp.bfloat16),
        in_specs=[whole(pltpu.SMEM), whole(pltpu.SMEM), whole(), whole()],
        out_specs=whole(),
        scratch_shapes=[
            pltpu.VMEM((2 * other.shape[0], HALF), jnp.float32),
            pltpu.VMEM((2 * back.shape[0], HALF), jnp.float32),
        ]
        + [pltpu.VMEM((2 * rows, HALF), jnp.float32)] * lanes,
        compiler_params=params(),
        cost_estimate=cost(estimate),
        name="spread_rows",
    )(2 * slot, 2 * other_slot, other, back)


def absorb_kernel(steps, batch, unroll, place_ref, received_ref, out_ref, total_ref, wide_ref):
    chunk = pl.program_id(0)

    @pl.when(chunk == 0)
    def _():
        clear(total_ref)

    @pl.when(chunk < steps)
    def _():
        widen(received_ref, wide_ref)
        rows = received_ref.shape[0]

        def body(first):
            for start in range(0, unroll, batch):
                places = place_ref.at[pl.ds(chunk * rows + first + start, batch)]
                at = [row(places[j]) for j in range(batch)]
                values = [
                    total_ref[at[j], :] + wide_ref[row(2 * (first + start + j)), :]
                    for j in range(batch)
                ]
                for j in reversed(range(batch)):
                    total_ref[at[j], :] = values[j]

        loop(rows, unroll, body)

    @pl.when(chunk >= steps)
    def _():
        base = pl.multiple_of((chunk - steps) * out_ref.shape[0], out_ref.shape[0])

        def finish(first):
            out_ref[pl.ds(first, 64), :] = joined(total_ref, base + first, 64)

        loop(out_ref.shape[0], 64, finish)


def absorb_rows(index, received, held, batch=16, unroll=80):
    count, features = received.shape
    chunk, block = 2560, 2048
    steps = count // chunk
    return pl.pallas_call(
        functools.partial(absorb_kernel, steps, batch, unroll),
        grid=(steps + held // block,),
        out_shape=jax.ShapeDtypeStruct((held, features), jnp.float32),
        in_specs=[
            whole(pltpu.SMEM),
            pl.BlockSpec((chunk, features), lambda i: (jnp.minimum(i, steps - 1), 0)),
        ],
        out_specs=pl.BlockSpec((block, features), lambda i: (jnp.maximum(i - steps, 0), 0)),
        scratch_shapes=[
            pltpu.VMEM((2 * held, HALF), jnp.float32),
            pltpu.VMEM((2 * chunk, HALF), jnp.float32),
        ],
        compiler_params=params(),
        cost_estimate=cost(22),
        name="absorb_rows",
    )(2 * index, received)


def local(
    quotient,
    remainder,
    request_q,
    request_r,
    query_q,
    query_r,
    item_q,
    item_r,
    positive,
    query_w1,
    query_w2,
    query_w3,
    item_w1,
    item_w2,
    item_w3,
):
    features = quotient.shape[1]
    capacity_q = request_q.shape[2]
    examples = query_q.shape[0]
    lists = request_q.shape[1]
    group = lists // lax.axis_size("grp")
    asked = exchange(jnp.concatenate([request_q[0], request_r[0]], axis=1))
    asked_q = jnp.maximum(asked[:, :capacity_q], 0).reshape(-1)
    asked_r = asked[:, capacity_q:].reshape(-1)
    shard_r = remainder.shape[0]
    named_r = (asked_r[:, None] == jnp.arange(shard_r, dtype=jnp.int32)[None, :]).astype(
        jnp.bfloat16
    )
    served_r = jnp.dot(named_r, remainder, preferred_element_type=jnp.float32).astype(jnp.bfloat16)
    served_q = pick_rows(asked_q, quotient)
    table_r = exchange(served_r.reshape(lists, -1, features)).reshape(-1, features)
    table_q = exchange(served_q.reshape(lists, -1, features)).reshape(-1, features)

    slots_iq, slots_ir = item_q.reshape(-1), item_r.reshape(-1)
    slots_qq, slots_qr = query_q.reshape(-1), query_r.reshape(-1)
    slots_q = jnp.concatenate([slots_qq, slots_iq])
    slots_r = jnp.concatenate([slots_qr, slots_ir])
    pooled = pool_rows(slots_q, slots_r, table_q, table_r, 2 * examples)
    pooled_query, pooled_item = pooled[:examples], pooled[examples:]
    query_unit, query_saved = tower_forward(pooled_query, query_w1, query_w2, query_w3)
    item_unit, item_saved = tower_forward(pooled_item, item_w1, item_w2, item_w3)
    units = jnp.concatenate([item_unit, query_unit], axis=1)
    units_all = gather_group(units)
    items_all, queries_all = units_all[:, :features], units_all[:, features:]

    columns = jnp.arange(items_all.shape[0], dtype=jnp.int32)[None, :]
    weights = score_weights(query_unit, items_all)
    inverse = 1.0 / jnp.sum(weights, axis=1, keepdims=True)
    target = (positive[:, None] == columns).astype(jnp.float32)
    d_query = SCALE * jnp.dot(
        (weights * inverse - target).astype(jnp.bfloat16),
        items_all,
        preferred_element_type=jnp.float32,
    )
    told = jnp.stack([inverse[:, 0], positive.astype(jnp.float32)])
    told_all = lax.all_to_all(
        jnp.broadcast_to(told[None], (group, *told.shape)),
        GROUP_AXES,
        split_axis=0,
        concat_axis=0,
        tiled=True,
    )
    query_back, query_backs = tower_backward(d_query, query_saved, query_w1, query_w2, query_w3)
    told_all, query_backs = lax.optimization_barrier((told_all, query_backs))
    query_terms = core_sum(weight_grads(pooled_query, query_saved, query_backs))
    inverse_all, positive_all = (told_all[:, i, :].reshape(1, -1) for i in range(2))
    own = lax.axis_index(GROUP_AXES) * examples + jnp.arange(examples, dtype=jnp.int32)
    weights_t = score_weights(item_unit, queries_all)
    target_t = (positive_all == own[:, None].astype(jnp.float32)).astype(jnp.float32)
    d_item = SCALE * jnp.dot(
        (weights_t * inverse_all - target_t).astype(jnp.bfloat16),
        queries_all,
        preferred_element_type=jnp.float32,
    )
    item_back, item_backs = tower_backward(d_item, item_saved, item_w1, item_w2, item_w3)
    item_terms = core_sum(weight_grads(pooled_item, item_saved, item_backs))
    back_all = jnp.concatenate([query_back, item_back], axis=0)
    terms = jnp.concatenate([query_terms, item_terms], axis=2)
    back_all, terms = lax.optimization_barrier((back_all, terms))
    part = chip_sum(terms)
    sums_q = spread_rows(slots_q, slots_r, table_r, back_all, table_q.shape[0], 25)
    sums_r = spread_rows(slots_r, slots_q, table_q, back_all, table_r.shape[0], 25)
    sums_q, sums_r, part = lax.optimization_barrier((sums_q, sums_r, part))
    summed = gather_rows(part)
    back_q = exchange(sums_q.reshape(lists, -1, features)).reshape(-1, features)
    back_q, sums_r = lax.optimization_barrier((back_q, sums_r))
    back_r = exchange(sums_r.reshape(lists, -1, features)).reshape(-1, features)
    grad_quotient = absorb_rows(asked_q, back_q, quotient.shape[0])
    grad_quotient, back_r = lax.optimization_barrier((grad_quotient, back_r))
    grad_remainder = inner(named_r, back_r)
    grad_remainder, summed = lax.optimization_barrier((grad_remainder, summed))
    hidden = query_w2.shape[0]
    weights_out = []
    for both in jnp.split(summed, 2, axis=1):
        second, third, first_t = jnp.split(both, [hidden, hidden + features], axis=1)
        weights_out += [first_t.T, second, third]
    return (grad_quotient, grad_remainder, *weights_out)


def solution(mesh):
    cores = Mesh(mesh.devices.reshape(4, 4, 4, 2), MESH_AXES)
    rows = P(MESH_AXES)
    return jax.shard_map(
        local,
        mesh=cores,
        in_specs=(rows,) * 9 + (P(),) * 6,
        out_specs=(rows,) * 2 + (P(),) * 6,
        check_vma=False,
    )
```

```python
import functools

import jax
import jax.numpy as jnp
from jax import lax
from jax.experimental import pallas as pl
from jax.experimental.layout import Layout, with_layout_constraint
from jax.experimental.pallas import tpu as pltpu
from jax.sharding import Mesh
from jax.sharding import PartitionSpec as P

SCALE = 20.0
EPS = 1e-06
GROUP_AXES = ("z", "x", "core")
MESH_AXES = ("grp", "z", "x", "core")
CHIP_AXES = ("grp", "z", "x")
CORES = [(0, 1), (1, 0)]
VMEM_LIMIT = 60 * 1024 * 1024
HALF = 128


def inner(left, right):
    return lax.dot_general(
        left, right, (((0,), (0,)), ((), ())), preferred_element_type=jnp.float32
    )


def outer_t(left, right):
    return lax.dot_general(
        left, right, (((1,), (1,)), ((), ())), preferred_element_type=jnp.float32
    )


def gelu_back(pre_value, upstream):
    return jax.vjp(jax.nn.gelu, pre_value)[1](upstream)[0]


def tower_forward(pooled, first, second, third):
    pre_one = jnp.dot(pooled, first, preferred_element_type=jnp.float32)
    act_one = jax.nn.gelu(pre_one).astype(jnp.bfloat16)
    pre_two = jnp.dot(act_one, second, preferred_element_type=jnp.float32)
    act_two = jax.nn.gelu(pre_two).astype(jnp.bfloat16)
    vector = jnp.dot(act_two, third, preferred_element_type=jnp.float32)
    inv_norm = lax.rsqrt(jnp.sum(vector * vector, axis=1, keepdims=True) + EPS)
    unit_vec = (vector * inv_norm).astype(jnp.bfloat16)
    return (unit_vec, (pre_one, act_one, pre_two, act_two, vector, inv_norm))


def tower_backward(d_unit, saved, first, second, third):
    pre_one, act_one, pre_two, act_two, vector, inv_norm = saved
    along = jnp.sum(vector * d_unit, axis=1, keepdims=True)
    cubed = inv_norm * inv_norm * inv_norm
    d_vector = (inv_norm * d_unit - cubed * vector * along).astype(jnp.bfloat16)
    d_pre_two = gelu_back(pre_two, outer_t(d_vector, third)).astype(jnp.bfloat16)
    d_pre_one = gelu_back(pre_one, outer_t(d_pre_two, second)).astype(jnp.bfloat16)
    return outer_t(d_pre_one, first), (d_pre_one, d_pre_two, d_vector)


def weight_grads(pooled, saved, backs):
    act_one, act_two = saved[1], saved[3]
    d_pre_one, d_pre_two, d_vector = backs
    grads = (inner(act_one, d_pre_two), inner(act_two, d_vector), inner(d_pre_one, pooled))
    joint = jnp.concatenate([g.astype(jnp.bfloat16) for g in grads], axis=1)
    return with_layout_constraint(joint, Layout(major_to_minor=(0, 1)))


def score_weights(left, right):
    return jnp.exp(SCALE * outer_t(left, right) - SCALE)


def gather_group(values):
    return lax.all_gather(values, GROUP_AXES, axis=0, tiled=True)


def exchange(rows):
    return lax.all_to_all(rows, MESH_AXES, split_axis=0, concat_axis=0, tiled=True)


def core_sum(grads):
    core, half = lax.axis_index("core"), grads.shape[0] // 2
    kept = lax.dynamic_slice_in_dim(grads, core * half, half, 0)
    given = lax.dynamic_slice_in_dim(grads, (1 - core) * half, half, 0)
    got = lax.ppermute(given, "core", CORES)
    chips = lax.axis_size(CHIP_AXES)
    both = kept.astype(jnp.float32) + got.astype(jnp.float32)
    return both.astype(jnp.bfloat16).reshape(chips, half // chips, -1)


def chip_sum(terms):
    terms = lax.all_to_all(terms, CHIP_AXES, split_axis=0, concat_axis=0, tiled=True)
    return jnp.sum(terms.astype(jnp.float32), axis=0).astype(jnp.bfloat16)


def gather_rows(part):
    return lax.all_gather(part, ("core", *CHIP_AXES), axis=0, tiled=True)


def cost(microseconds):
    return pl.CostEstimate(flops=0, bytes_accessed=int(microseconds * 3.6e6), transcendentals=0)


def whole(space=pltpu.VMEM):
    return pl.BlockSpec(memory_space=space)


def params():
    return pltpu.CompilerParams(vmem_limit_bytes=VMEM_LIMIT)


def loop(count, step, body):
    def run(i, carry):
        body(pl.multiple_of(i * step, step))
        return carry

    lax.fori_loop(0, count // step, run, 0)


def row(place):
    return pl.ds(pl.multiple_of(place, 2), 2)


def halves(first, rows):
    place = pl.multiple_of(2 * first, 16)
    return pl.ds(place, rows, stride=2), pl.ds(place + 1, rows, stride=2)


def widen(narrow_ref, wide_ref, step=64):
    def body(first):
        value = narrow_ref[pl.ds(first, step), :].astype(jnp.float32)
        left, right = halves(first, step)
        wide_ref[left, :] = value[:, :HALF]
        wide_ref[right, :] = value[:, HALF:]

    loop(narrow_ref.shape[0], step, body)


def joined(wide_ref, first, rows):
    left, right = halves(first, rows)
    return jnp.concatenate([wide_ref[left, :], wide_ref[right, :]], axis=1)


def clear(*refs):
    def body(first):
        for ref in refs:
            ref[pl.ds(first, 128), :] = jnp.zeros((128, HALF), jnp.float32)

    loop(refs[0].shape[0], 128, body)


def pick_kernel(place_ref, table_ref, out_ref, wide_ref, stage_ref):
    rows = out_ref.shape[0]
    group = stage_ref.shape[0] // 2
    chunk = pl.program_id(0)

    @pl.when(chunk == 0)
    def _():
        widen(table_ref, wide_ref)

    def body(first):
        places = place_ref.at[pl.ds(chunk * rows + first, group)]
        for j in range(group):
            stage_ref[pl.ds(2 * j, 2), :] = wide_ref[row(places[j]), :]
        out_ref[pl.ds(first, group), :] = joined(stage_ref, 0, group).astype(jnp.bfloat16)

    loop(rows, group, body)


def pick_rows(index, table, chunk=2048, group=64):
    count, (held, features) = index.shape[0], table.shape
    return pl.pallas_call(
        pick_kernel,
        grid=(count // chunk,),
        out_shape=jax.ShapeDtypeStruct((count, features), jnp.bfloat16),
        in_specs=[whole(pltpu.SMEM), whole()],
        out_specs=pl.BlockSpec((chunk, features), lambda i: (i, 0)),
        scratch_shapes=[
            pltpu.VMEM((2 * held, HALF), jnp.float32),
            pltpu.VMEM((2 * group, HALF), jnp.float32),
        ],
        compiler_params=params(),
        cost_estimate=cost(12),
        name="pick_rows",
    )(2 * index, table)


def pool_kernel(place_q_ref, place_r_ref, table_q_ref, table_r_ref, out_ref, wide_q, wide_r, stage_ref):
    widen(table_r_ref, wide_r)
    widen(table_q_ref, wide_q)
    examples = out_ref.shape[0]
    bag = place_q_ref.shape[0] // examples
    group = stage_ref.shape[0] // 2

    def body(first):
        for j in range(group):
            place = (first + j) * bag
            total = None
            for l in range(bag):
                left = wide_q[row(place_q_ref[place + l]), :]
                term = left * wide_r[row(place_r_ref[place + l]), :]
                total = term if total is None else total + term
            stage_ref[pl.ds(2 * j, 2), :] = total
        out_ref[pl.ds(first, group), :] = joined(stage_ref, 0, group).astype(jnp.bfloat16)

    loop(examples, group, body)


def pool_rows(slot_q, slot_r, table_q, table_r, examples, group=16):
    features = table_q.shape[1]
    return pl.pallas_call(
        pool_kernel,
        out_shape=jax.ShapeDtypeStruct((examples, features), jnp.bfloat16),
        in_specs=[whole(pltpu.SMEM), whole(pltpu.SMEM), whole(), whole()],
        out_specs=whole(),
        scratch_shapes=[
            pltpu.VMEM((2 * table_q.shape[0], HALF), jnp.float32),
            pltpu.VMEM((2 * table_r.shape[0], HALF), jnp.float32),
            pltpu.VMEM((2 * group, HALF), jnp.float32),
        ],
        compiler_params=params(),
        cost_estimate=cost(18),
        name="pool_rows",
    )(2 * slot_q, 2 * slot_r, table_q, table_r)


def spread_kernel(place_ref, other_place_ref, other_ref, back_ref, out_ref, wide_ref, back_wide, *totals):
    widen(other_ref, wide_ref)
    widen(back_ref, back_wide)
    clear(*totals)
    examples = back_ref.shape[0]
    bag = place_ref.shape[0] // examples
    share = examples // len(totals)

    def body(e):
        lanes = []
        for lane, total in enumerate(totals):
            example = lane * share + e
            bag_at = pl.ds(example * bag, bag)
            back = back_wide[row(2 * example), :]
            lanes.append((total, back, place_ref.at[bag_at], other_place_ref.at[bag_at]))
        for l in range(bag):
            for total, back, places, other_places in lanes:
                at = row(places[l])
                total[at, :] = total[at, :] + back * wide_ref[row(other_places[l]), :]

    loop(share, 1, body)

    def finish(first):
        value = joined(totals[0], first, 64)
        for total in totals[1:]:
            value = value + joined(total, first, 64)
        out_ref[pl.ds(first, 64), :] = value.astype(jnp.bfloat16)

    loop(out_ref.shape[0], 64, finish)


def spread_rows(slot, other_slot, other, back, rows, estimate, lanes=4):
    features = other.shape[1]
    return pl.pallas_call(
        spread_kernel,
        out_shape=jax.ShapeDtypeStruct((rows, features), jnp.bfloat16),
        in_specs=[whole(pltpu.SMEM), whole(pltpu.SMEM), whole(), whole()],
        out_specs=whole(),
        scratch_shapes=[
            pltpu.VMEM((2 * other.shape[0], HALF), jnp.float32),
            pltpu.VMEM((2 * back.shape[0], HALF), jnp.float32),
        ]
        + [pltpu.VMEM((2 * rows, HALF), jnp.float32)] * lanes,
        compiler_params=params(),
        cost_estimate=cost(estimate),
        name="spread_rows",
    )(2 * slot, 2 * other_slot, other, back)


def absorb_kernel(steps, batch, unroll, place_ref, received_ref, out_ref, total_ref, wide_ref):
    chunk = pl.program_id(0)

    @pl.when(chunk == 0)
    def _():
        clear(total_ref)

    @pl.when(chunk < steps)
    def _():
        widen(received_ref, wide_ref)
        rows = received_ref.shape[0]

        def body(first):
            for start in range(0, unroll, batch):
                places = place_ref.at[pl.ds(chunk * rows + first + start, batch)]
                at = [row(places[j]) for j in range(batch)]
                values = [
                    total_ref[at[j], :] + wide_ref[row(2 * (first + start + j)), :]
                    for j in range(batch)
                ]
                for j in reversed(range(batch)):
                    total_ref[at[j], :] = values[j]

        loop(rows, unroll, body)

    @pl.when(chunk >= steps)
    def _():
        base = pl.multiple_of((chunk - steps) * out_ref.shape[0], out_ref.shape[0])

        def finish(first):
            out_ref[pl.ds(first, 64), :] = joined(total_ref, base + first, 64)

        loop(out_ref.shape[0], 64, finish)


def absorb_rows(index, received, held, batch=16, unroll=80):
    count, features = received.shape
    chunk, block = 2560, 2048
    steps = count // chunk
    return pl.pallas_call(
        functools.partial(absorb_kernel, steps, batch, unroll),
        grid=(steps + held // block,),
        out_shape=jax.ShapeDtypeStruct((held, features), jnp.float32),
        in_specs=[
            whole(pltpu.SMEM),
            pl.BlockSpec((chunk, features), lambda i: (jnp.minimum(i, steps - 1), 0)),
        ],
        out_specs=pl.BlockSpec((block, features), lambda i: (jnp.maximum(i - steps, 0), 0)),
        scratch_shapes=[
            pltpu.VMEM((2 * held, HALF), jnp.float32),
            pltpu.VMEM((2 * chunk, HALF), jnp.float32),
        ],
        compiler_params=params(),
        cost_estimate=cost(22),
        name="absorb_rows",
    )(2 * index, received)


def local(
    quotient,
    remainder,
    request_q,
    request_r,
    query_q,
    query_r,
    item_q,
    item_r,
    positive,
    query_w1,
    query_w2,
    query_w3,
    item_w1,
    item_w2,
    item_w3,
):
    features = quotient.shape[1]
    capacity_q = request_q.shape[2]
    examples = query_q.shape[0]
    lists = request_q.shape[1]
    group = lists // lax.axis_size("grp")
    asked = exchange(jnp.concatenate([request_q[0], request_r[0]], axis=1))
    asked_q = jnp.maximum(asked[:, :capacity_q], 0).reshape(-1)
    asked_r = asked[:, capacity_q:].reshape(-1)
    shard_r = remainder.shape[0]
    named_r = (asked_r[:, None] == jnp.arange(shard_r, dtype=jnp.int32)[None, :]).astype(
        jnp.bfloat16
    )
    served_r = jnp.dot(named_r, remainder, preferred_element_type=jnp.float32).astype(jnp.bfloat16)
    served_q = pick_rows(asked_q, quotient)
    table_r = exchange(served_r.reshape(lists, -1, features)).reshape(-1, features)
    table_q = exchange(served_q.reshape(lists, -1, features)).reshape(-1, features)

    slots_iq, slots_ir = item_q.reshape(-1), item_r.reshape(-1)
    slots_qq, slots_qr = query_q.reshape(-1), query_r.reshape(-1)
    slots_q = jnp.concatenate([slots_qq, slots_iq])
    slots_r = jnp.concatenate([slots_qr, slots_ir])
    pooled = pool_rows(slots_q, slots_r, table_q, table_r, 2 * examples)
    pooled_query, pooled_item = pooled[:examples], pooled[examples:]
    query_unit, query_saved = tower_forward(pooled_query, query_w1, query_w2, query_w3)
    item_unit, item_saved = tower_forward(pooled_item, item_w1, item_w2, item_w3)
    units = jnp.concatenate([item_unit, query_unit], axis=1)
    units_all = gather_group(units)
    items_all, queries_all = units_all[:, :features], units_all[:, features:]

    columns = jnp.arange(items_all.shape[0], dtype=jnp.int32)[None, :]
    weights = score_weights(query_unit, items_all)
    inverse = 1.0 / jnp.sum(weights, axis=1, keepdims=True)
    target = (positive[:, None] == columns).astype(jnp.float32)
    d_query = SCALE * jnp.dot(
        (weights * inverse - target).astype(jnp.bfloat16),
        items_all,
        preferred_element_type=jnp.float32,
    )
    told = jnp.stack([inverse[:, 0], positive.astype(jnp.float32)])
    told_all = lax.all_to_all(
        jnp.broadcast_to(told[None], (group, *told.shape)),
        GROUP_AXES,
        split_axis=0,
        concat_axis=0,
        tiled=True,
    )
    query_back, query_backs = tower_backward(d_query, query_saved, query_w1, query_w2, query_w3)
    weights_t = score_weights(item_unit, queries_all)
    told_all, query_backs, weights_t = lax.optimization_barrier((told_all, query_backs, weights_t))
    query_terms = core_sum(weight_grads(pooled_query, query_saved, query_backs))
    inverse_all, positive_all = (told_all[:, i, :].reshape(1, -1) for i in range(2))
    own = lax.axis_index(GROUP_AXES) * examples + jnp.arange(examples, dtype=jnp.int32)
    target_t = (positive_all == own[:, None].astype(jnp.float32)).astype(jnp.float32)
    d_item = SCALE * jnp.dot(
        (weights_t * inverse_all - target_t).astype(jnp.bfloat16),
        queries_all,
        preferred_element_type=jnp.float32,
    )
    item_back, item_backs = tower_backward(d_item, item_saved, item_w1, item_w2, item_w3)
    item_terms = core_sum(weight_grads(pooled_item, item_saved, item_backs))
    back_all = jnp.concatenate([query_back, item_back], axis=0)
    terms = jnp.concatenate([query_terms, item_terms], axis=2)
    back_all, terms = lax.optimization_barrier((back_all, terms))
    part = chip_sum(terms)
    sums_q = spread_rows(slots_q, slots_r, table_r, back_all, table_q.shape[0], 25)
    sums_r = spread_rows(slots_r, slots_q, table_q, back_all, table_r.shape[0], 25)
    sums_q, sums_r, part = lax.optimization_barrier((sums_q, sums_r, part))
    summed = gather_rows(part)
    back_q = exchange(sums_q.reshape(lists, -1, features)).reshape(-1, features)
    back_q, sums_r = lax.optimization_barrier((back_q, sums_r))
    back_r = exchange(sums_r.reshape(lists, -1, features)).reshape(-1, features)
    grad_quotient = absorb_rows(asked_q, back_q, quotient.shape[0])
    grad_quotient, back_r = lax.optimization_barrier((grad_quotient, back_r))
    grad_remainder = inner(named_r, back_r)
    grad_remainder, summed = lax.optimization_barrier((grad_remainder, summed))
    hidden = query_w2.shape[0]
    weights_out = []
    for both in jnp.split(summed, 2, axis=1):
        second, third, first_t = jnp.split(both, [hidden, hidden + features], axis=1)
        weights_out += [first_t.T, second, third]
    return (grad_quotient, grad_remainder, *weights_out)


def solution(mesh):
    cores = Mesh(mesh.devices.reshape(4, 4, 4, 2), MESH_AXES)
    rows = P(MESH_AXES)
    return jax.shard_map(
        local,
        mesh=cores,
        in_specs=(rows,) * 9 + (P(),) * 6,
        out_specs=(rows,) * 2 + (P(),) * 6,
        check_vma=False,
    )
```
